32 devices in a mesh: fsdp: 2 (over y), context: 4 (over x, core), tensor: 4 (over z).
Axes of the slice: x: 2, y: 2, z: 4, core: 2. Of those that a mesh axis runs over, the one named last changes fastest.
Arguments:
- tokens: bfloat16 [4, 2048, 2048], P('fsdp', 'context'), may hold values from -6 to 6
- ln_gain: bfloat16 [2048], P('fsdp'), may hold values from 0.5 to 1.5
- ln_bias: bfloat16 [2048], P('fsdp'), may hold values from -1.796875 to 1.796875
- w_qkv: bfloat16 [3, 2048, 2048], P(None, 'fsdp', 'tensor'), may hold values from -0.1875 to 0.1875
- b_qkv: bfloat16 [3, 2048], P(None, ('tensor', 'fsdp')), may hold values from -3 to 3
- w_out: bfloat16 [2048, 2048], P('tensor', 'fsdp'), may hold values from -0.5 to 0.5
- b_out: bfloat16 [2048], P('fsdp'), may hold values from -1.796875 to 1.796875
- w_fc1: bfloat16 [2048, 8192], P('fsdp', 'tensor'), may hold values from -0.125 to 0.125
- b_fc1: bfloat16 [8192], P(('tensor', 'fsdp')), may hold values from -3 to 3
- w_fc2: bfloat16 [8192, 2048], P('tensor', 'fsdp'), may hold values from -0.09375 to 0.09375
- b_fc2: bfloat16 [2048], P('fsdp'), may hold values from -1.796875 to 1.796875
- cotangent: bfloat16 [4, 2048, 2048], P('fsdp', 'context'), may hold values from -6 to 6
Outputs:
- block_out: bfloat16 [4, 2048, 2048], P('fsdp', 'context')
- tokens_grad: bfloat16 [4, 2048, 2048], P('fsdp', 'context')
- ln_gain_grad: float32 [2048], P('fsdp')
- ln_bias_grad: float32 [2048], P('fsdp')
- w_qkv_grad: float32 [3, 2048, 2048], P(None, 'fsdp', 'tensor')
- b_qkv_grad: float32 [3, 2048], P(None, ('tensor', 'fsdp'))
- w_out_grad: float32 [2048, 2048], P('tensor', 'fsdp')
- b_out_grad: float32 [2048], P('fsdp')
- w_fc1_grad: float32 [2048, 8192], P('fsdp', 'tensor')
- b_fc1_grad: float32 [8192], P(('tensor', 'fsdp'))
- w_fc2_grad: float32 [8192, 2048], P('tensor', 'fsdp')
- b_fc2_grad: float32 [2048], P('fsdp')
The draws below stay inside these ranges and needn't reach their ends.
All inputs are finite; a program needn't handle non-finite values.
Results may differ from the reference program's by a relative error of at most 0.012.
The reference program's roundings to bfloat16 on the way count: a program that leaves them out, or rounds other values in their place, can miss the bound.
Values may be sent and summed in bfloat16 or wider, within the bound.
No kernel may reach another device: no remote copies, remote signals or barrier semaphores. Data moves between devices by JAX's collectives and lax.ppermute only.
A program may use at most 256 MiB of HBM per device.

```python
import jax
import jax.numpy as jnp
from jax import lax

D = 2048
H = 32
HD = 64
ROT = 32
FF = 8192
LENGTH = 2048
BATCH = 4


def shard_levels(rng, extent, shards, low, high):
    def one(position, shards_of):
        heights = jax.random.uniform(jax.random.fold_in(jax.random.fold_in(rng, 6), position), (shards_of,), jnp.float32, low / len(shards), high / len(shards))
        return jnp.repeat(jnp.exp(heights), extent[position] // shards_of).reshape((-1,) + (1,) * (len(extent) - position - 1))

    factor_of = one(*shards[0])
    for cut in shards[1:]:
        factor_of = factor_of * one(*cut)
    return factor_of


def scatter_about(rng, dims, scale, reach, pieces=(), dtype=jnp.bfloat16):
    result = scale * jax.random.normal(rng, dims, jnp.float32)
    if pieces:
        result = result * shard_levels(rng, dims, pieces, -0.22, 0.18)
    return jnp.clip(result, -reach, reach).astype(dtype)


def setup_inputs(seed: int = 0) -> dict:
    streams_of = jax.random.split(jax.random.key(seed), 13)
    return {
        "tokens": scatter_about(streams_of[0], (BATCH, LENGTH, D), 1.0, 6.0, ((0, 2), (1, 4))),
        "ln_gain": jnp.clip(1.0 + 0.1 * jax.random.normal(streams_of[1], (D,), jnp.float32), 0.5, 1.5).astype(jnp.bfloat16),
        "ln_bias": scatter_about(streams_of[2], (D,), 0.3, 1.796875, ((0, 2),)),
        "w_qkv": scatter_about(streams_of[3], (3, D, D), (D // 2) ** -0.5, 0.1875, ((1, 2), (2, 4))),
        "b_qkv": scatter_about(streams_of[4], (3, D), 0.5, 3.0, ((1, 8),)),
        "w_out": scatter_about(streams_of[5], (D, D), (D // 16) ** -0.5, 0.5, ((0, 4), (1, 2))),
        "b_out": scatter_about(streams_of[6], (D,), 0.3, 1.796875, ((0, 2),)),
        "w_fc1": scatter_about(streams_of[7], (D, FF), D ** -0.5, 0.125, ((0, 2), (1, 4))),
        "b_fc1": scatter_about(streams_of[8], (FF,), 0.5, 3.0, ((0, 8),)),
        "w_fc2": scatter_about(streams_of[9], (FF, D), (FF // 2) ** -0.5, 0.09375, ((0, 4), (1, 2))),
        "b_fc2": scatter_about(streams_of[10], (D,), 0.3, 1.796875, ((0, 2),)),
        "cotangent": scatter_about(streams_of[11], (BATCH, LENGTH, D), 1.0, 6.0, ((0, 2), (1, 4))),
    }


@jax.custom_vjp
def low(v):
    return lax.optimization_barrier(v.astype(jnp.bfloat16)).astype(jnp.float32)

@jax.custom_vjp
def low_back(v):
    return v

def low_keep(v):
    return (low(v), None)

def low_pass(kept, grad):
    return (grad,)

def back_keep(v):
    return (v, None)

def back_low(kept, grad):
    return (low(grad),)
low.defvjp(low_keep, low_pass)
low_back.defvjp(back_keep, back_low)
EPSILON = 1e-05
HIGHEST = lax.Precision.HIGHEST

def layer_norm(values, norm_gain, norm_bias):
    centered = values - lax.optimization_barrier(jnp.mean(values, -1, keepdims=True))
    variance = lax.optimization_barrier(jnp.mean(centered * centered, -1, keepdims=True))
    return centered * lax.rsqrt(variance + EPSILON) * norm_gain + norm_bias

def rotation_tables(positions):
    half_rot = ROT // 2
    exponents = jnp.arange(half_rot).astype(jnp.float32) * (2.0 / ROT)
    inverse = jnp.power(10000.0, -exponents)
    angles = positions[:, None] * inverse[None, :]
    return (jnp.cos(angles), jnp.sin(angles))

def rotate(field, cosine, sine):
    half_rot = ROT // 2
    first = field[..., :half_rot]
    second = field[..., half_rot:ROT]
    return jnp.concatenate([first * cosine - second * sine, second * cosine + first * sine, field[..., ROT:]], -1)

def head_attend(stacked):
    query = stacked[0]
    key = stacked[1]
    value = stacked[2]
    length = query.shape[0]
    scores = low_back(jnp.dot(query, key.T, precision=HIGHEST) * HD ** (-0.5))
    places = jnp.arange(length)
    allowed = places[None, :] <= places[:, None]
    scores = jnp.where(allowed, scores, -1e+30)
    probs = jax.nn.softmax(scores, axis=-1)
    return jnp.dot(low(probs), value, precision=HIGHEST)

def sequence_forward(params, sequence):
    norm_gain, norm_bias, qkv_weight, qkv_bias, out_weight, out_bias, fc1_weight, fc1_bias, fc2_weight, fc2_bias = params
    length = sequence.shape[0]
    normed = low(layer_norm(sequence, norm_gain, norm_bias))
    raw = jnp.einsum('ld,cde->lce', normed, qkv_weight, precision=HIGHEST) + qkv_bias[None, :, :]
    raw = low_back(raw)
    heads = raw.reshape(length, 3, H, HD)
    cosine, sine = rotation_tables(jnp.arange(length).astype(jnp.float32))
    turned_qk = rotate(heads[:, :2], cosine[:, None, None, :], sine[:, None, None, :])
    turned = low(low_back(jnp.concatenate([turned_qk, heads[:, 2:]], 1)))
    per_head = jnp.transpose(turned, (2, 1, 0, 3))
    context = lax.map(jax.checkpoint(head_attend), per_head)
    context = low(low_back(context))
    merged = jnp.transpose(context, (1, 0, 2)).reshape(length, D)
    attended = jnp.dot(merged, out_weight, precision=HIGHEST) + out_bias
    pre = low_back(jnp.dot(normed, fc1_weight, precision=HIGHEST) + fc1_bias)
    hidden = low(jax.nn.gelu(pre, approximate=True))
    fed = jnp.dot(hidden, fc2_weight, precision=HIGHEST) + fc2_bias
    return sequence + attended + fed

def reference(tokens, ln_gain, ln_bias, w_qkv, b_qkv, w_out, b_out, w_fc1, b_fc1, w_fc2, b_fc2, cotangent):
    params = (ln_gain.astype(jnp.float32), ln_bias.astype(jnp.float32), w_qkv.astype(jnp.float32), b_qkv.astype(jnp.float32), w_out.astype(jnp.float32), b_out.astype(jnp.float32), w_fc1.astype(jnp.float32), b_fc1.astype(jnp.float32), w_fc2.astype(jnp.float32), b_fc2.astype(jnp.float32))
    inputs = tokens.astype(jnp.float32)

    def forward(values, weights):

        def one_sequence(sequence):
            return sequence_forward(weights, sequence)
        return lax.map(jax.checkpoint(one_sequence), values)
    outputs, pullback = jax.vjp(forward, inputs, params)
    input_grad, weight_grads = pullback(cotangent.astype(jnp.float32))
    return (outputs.astype(jnp.bfloat16), input_grad.astype(jnp.bfloat16), weight_grads[0], weight_grads[1], weight_grads[2], weight_grads[3], weight_grads[4], weight_grads[5], weight_grads[6], weight_grads[7], weight_grads[8], weight_grads[9])
```

```python
import functools

import jax
import jax.numpy as jnp
from jax import lax
import jax.experimental.pallas as pl
import jax.experimental.pallas.tpu as pltpu
from jax.sharding import PartitionSpec as P

HD = 64
ROT = 32
EPSILON = 1e-05
LANES = 128
F32 = jnp.float32
BF16 = jnp.bfloat16
ROOT = 0.7978845608028654
CUBE = 0.044715
VMEM_BYTES = 60 << 20


def lasting(micros):
    return pl.CostEstimate(flops=0, bytes_accessed=int(micros * 3.4e6), transcendentals=0)


def nn(a, b):
    return lax.dot_general(a, b, (((1,), (0,)), ((), ())), preferred_element_type=F32)


def nt(a, b):
    return lax.dot_general(a, b, (((1,), (1,)), ((), ())), preferred_element_type=F32)


def tn(a, b):
    return lax.dot_general(a, b, (((0,), (0,)), ((), ())), preferred_element_type=F32)


def add_low(*terms):
    total = terms[0].astype(F32)
    for term in terms[1:]:
        total = total + term.astype(F32)
    return total.astype(BF16)


def to_fsdp(value):
    return lax.ppermute(value, "fsdp", [(0, 1), (1, 0)])


def to_context(value, mask):
    size = lax.axis_size("context")
    return lax.ppermute(value, "context", [(i, i ^ mask) for i in range(size)])


def to_tensor(value, mask):
    size = lax.axis_size("tensor")
    return lax.ppermute(value, "tensor", [(i, i ^ mask) for i in range(size)])


def after(value, *others):
    return lax.optimization_barrier((value,) + others)[0]


def masks_of(size):
    mask = 1
    while mask < size:
        yield mask
        mask *= 2


def sum_everywhere(value, over_tensor):
    for mask in masks_of(lax.axis_size("context")):
        value = value + to_context(value, mask)
    value = value + to_fsdp(value)
    if over_tensor:
        for mask in masks_of(lax.axis_size("tensor")):
            value = value + to_tensor(value, mask)
    return value


def own_blocks(own, axis, place, block):
    count = own.shape[axis] // block
    return [
        lax.dynamic_slice_in_dim(own, (p ^ place) * block, block, axis) for p in range(count)
    ]


class Order:
    def __init__(self):
        self.last = None

    def __call__(self, value):
        return value if self.last is None else after(value, self.last)

    def mark(self, value):
        self.last = value
        return value

    def wait(self, *values):
        if self.last is not None:
            values = lax.optimization_barrier(values + (self.last,))[:-1]
        else:
            values = lax.optimization_barrier(values)
        self.last = values[0]
        return values


class Reduction:
    def __init__(self, order, pairs, block):
        self.order, self.pairs, self.block = order, pairs, block

    def send(self):
        (self.sent,) = outer(self.order, self.pairs, 1, None)
        self.sent = to_context(self.sent, 1)

    def keep(self):
        results = outer(self.order, self.pairs, 0, self.sent)
        self.near, self.far = results[: len(self.pairs)], results[len(self.pairs) :]
        self.near, self.far = list(self.near), list(self.far)
        self.pieces = [None] * len(self.pairs)

    def over_fsdp(self, i, *earlier):
        self.far[i] = to_fsdp(after(self.far[i], *earlier) if earlier else self.far[i])
        return self.far[i]

    def over_chips(self, i):
        self.near[i] = self.order.mark(add_low(self.order(self.near[i]), self.far[i]))
        self.masks = list(masks_of(lax.axis_size("context") // 2))
        if self.masks:
            self.far[i] = to_context(self.near[i], 2 * self.masks[0])
        return self.far[i]

    def over_cores(self, i):
        total = self.near[i]
        for n, mask in enumerate(self.masks):
            other = self.far[i] if n == 0 else to_context(total, 2 * mask)
            total = self.order.mark(add_turned(self.order(total), other, mask, self.block))
        self.pieces[i] = (total, to_context(total, 1))


def prepare_kernel(count, me_ref, tokens, grad, gain, bias, normed_out, grad_out, sum_out, kept):
    values = tokens[...].astype(F32)
    centered = values - jnp.mean(values, -1, keepdims=True)
    variance = jnp.mean(centered * centered, -1, keepdims=True)
    kept[...] = (centered * lax.rsqrt(variance + EPSILON) * gain[...] + bias[...]).astype(BF16)
    me = me_ref[0]
    block = tokens.shape[1] // count
    for p in range(count):
        source = pl.ds(pl.multiple_of((p ^ me) * block, block), block)
        normed_out[:, p * block : (p + 1) * block] = kept[:, source]
        grad_out[:, p * block : (p + 1) * block] = grad[:, source]
    part = jnp.sum(grad[...].astype(F32), 0, keepdims=True)

    @pl.when(pl.program_id(0) == 0)
    def _():
        sum_out[...] = part

    @pl.when(pl.program_id(0) > 0)
    def _():
        sum_out[...] += part


def prepare(me, count, tokens, grad, gain, bias):
    rows, width = tokens.shape
    tile = min(128, rows)
    row_spec = pl.BlockSpec((tile, width), lambda r, me: (r, 0))
    one_spec = pl.BlockSpec((1, width), lambda r, me: (0, 0))
    return pl.pallas_call(
        functools.partial(prepare_kernel, count),
        out_shape=[
            jax.ShapeDtypeStruct((rows, width), BF16),
            jax.ShapeDtypeStruct((rows, width), BF16),
            jax.ShapeDtypeStruct((1, width), F32),
        ],
        grid_spec=pltpu.PrefetchScalarGridSpec(
            num_scalar_prefetch=1,
            grid=(rows // tile,),
            in_specs=[row_spec, row_spec, one_spec, one_spec],
            out_specs=[row_spec, row_spec, one_spec],
            scratch_shapes=[pltpu.VMEM((tile, width), BF16)],
        ),
        compiler_params=pltpu.CompilerParams(vmem_limit_bytes=VMEM_BYTES),
        cost_estimate=lasting(10),
        name="prepare",
    )(me, tokens, grad, gain, bias)


def turn(part, cosine, below, above):
    return (
        part * cosine
        + pltpu.roll(part, LANES - ROT // 2, 1) * below
        + pltpu.roll(part, ROT // 2, 1) * above
    )


def project_kernel(seqs, qkv_count, out_count, parts, k_ref, c_ref, *refs):
    normed, grad, bias, cosine, below, above = refs[:6]
    ends = (6 + qkv_count, 6 + qkv_count + out_count)
    outs, kept = refs[ends[1] : -1], refs[-1]
    which = pl.program_id(0)
    rows, width = kept.shape
    length = rows // seqs

    @pl.when(which < 3)
    def _():
        weight = jnp.concatenate([w[0] for w in refs[6 : ends[0]]], 0)
        raw = nn(normed[...], weight) + bias[0]

        @pl.when(which < 2)
        def _():
            for s in range(seqs):
                for lane in range(0, width, LANES):
                    part = raw[s * length : (s + 1) * length, lane : lane + LANES]
                    kept[s * length : (s + 1) * length, lane : lane + LANES] = turn(
                        part, cosine[...], below[...], above[...]
                    ).astype(BF16)

        @pl.when(which == 2)
        def _():
            kept[...] = raw.astype(BF16)

    @pl.when(which == 3)
    def _():
        weight = jnp.concatenate([w[...] for w in refs[ends[0] : ends[1]]], 1)
        kept[...] = nt(grad[...], weight).astype(BF16)

    span = width // parts
    for m in range(parts):
        at = pl.ds(pl.multiple_of((m ^ c_ref[0]) * span, span), span) if parts > 1 else slice(None)
        for s in range(seqs):
            part = kept[s * length : (s + 1) * length, at]
            if parts == 1:
                outs[s][0, 0] = part
            else:
                outs[3 * s + min(m, 2)][max(m - 2, 0), 0] = part


def project(place, context, normed, grad, qkv, qkv_rest, out, out_rest, bias, tables, seqs, parts):
    rows, depth = normed.shape
    width = qkv.shape[2]
    block = qkv_rest[0].shape[1]
    count = qkv.shape[1] // block
    length = rows // seqs
    span = width // parts
    table = pl.BlockSpec((length, LANES), lambda c, k, x: (0, 0))
    whole = pl.BlockSpec((rows, depth), lambda c, k, x: (0, 0), pipeline_mode=pl.Buffered(1))

    def qkv_spec(p):
        return pl.BlockSpec((1, block, width), lambda c, k, x: (jnp.minimum(c, 2), p ^ k[0], 0))

    def out_spec(p):
        return pl.BlockSpec((width, block), lambda c, k, x: (0, p ^ k[0]))

    qkv_specs = [qkv_spec(p) for p in range(count)] + [
        pl.BlockSpec((1, block, width), lambda c, k, x: (jnp.minimum(c, 2), 0, 0))
    ] * len(qkv_rest)
    out_specs = [out_spec(p) for p in range(count)] + [
        pl.BlockSpec((width, block), lambda c, k, x: (0, 0))
    ] * len(out_rest)
    counts = [1] if parts == 1 else [1, 1, 2]
    results = pl.pallas_call(
        functools.partial(project_kernel, seqs, len(qkv_specs), len(out_specs), parts),
        out_shape=[jax.ShapeDtypeStruct((n, 4, length, span), BF16) for n in counts] * seqs,
        grid_spec=pltpu.PrefetchScalarGridSpec(
            num_scalar_prefetch=2,
            grid=(4,),
            in_specs=[
                whole,
                whole,
                pl.BlockSpec((1, 1, width), lambda c, k, x: (jnp.minimum(c, 2), 0, 0)),
                table,
                table,
                table,
            ]
            + qkv_specs
            + out_specs,
            out_specs=[
                pl.BlockSpec((n, 1, length, span), lambda c, k, x: (0, c, 0, 0)) for n in counts
            ]
            * seqs,
            scratch_shapes=[pltpu.VMEM((rows, width), BF16)],
        ),
        compiler_params=pltpu.CompilerParams(vmem_limit_bytes=VMEM_BYTES),
        cost_estimate=lasting(19),
        name="project",
    )(
        place,
        context,
        normed,
        grad,
        bias,
        *tables,
        *([qkv] * count),
        *qkv_rest,
        *([out] * count),
        *out_rest,
    )
    return [results[s * len(counts) : (s + 1) * len(counts)] for s in range(seqs)]


def attend_kernel(parts, queries_at_once, keys_at_once, me_ref, *refs):
    pieces = refs[:parts]
    outs = refs[parts:-11]
    q_all, k_all, v_all, g_all, v_turned, k_turned, o_all, dq_all, dk_all, dv_all, held = refs[-11:]
    rows, width = pieces[0].shape[2:]
    length = rows * parts
    me = me_ref[0]
    bq, bk = queries_at_once, keys_at_once
    scale = HD**-0.5
    for m in range(parts):
        at = pl.ds(pl.multiple_of((me ^ m) * rows, rows), rows)
        q_all[at, :] = (pieces[m][0, 0].astype(F32) * scale).astype(BF16)
        k_all[at, :] = pieces[m][0, 1]
        v_all[at, :] = pieces[m][0, 2]
        g_all[at, :] = pieces[m][0, 3]
    v_turned[...] = v_all[...].T
    k_turned[...] = k_all[...].T
    dk_all[...] = jnp.zeros_like(dk_all)
    dv_all[...] = jnp.zeros_like(dv_all)
    heads = width // HD
    lane_head = lax.broadcasted_iota(jnp.int32, (1, width), 1) // HD
    row_head = lax.broadcasted_iota(jnp.int32, (width, 1), 0) // HD

    def one_block(i, _):
        at_q = pl.ds(pl.multiple_of(i * bq, bq), bq)
        query = q_all[at_q, :]
        grad = g_all[at_q, :]
        blocks = (i + 1) * (bq // bk)
        outs_now = jnp.zeros((width, bq), F32)
        grads_now = jnp.zeros((width, bq), F32)
        for h in range(heads):
            q_head = jnp.where(lane_head == h, query, jnp.zeros_like(query))
            g_head = jnp.where(lane_head == h, grad, jnp.zeros_like(grad))

            def score(j, top, masked=False):
                at_k = pl.ds(pl.multiple_of(j * bk, bk), bk)
                scores = nt(k_all[at_k, :], q_head)
                if masked:
                    key = j * bk + lax.broadcasted_iota(jnp.int32, (bk, bq), 0)
                    place = i * bq + lax.broadcasted_iota(jnp.int32, (bk, bq), 1)
                    scores = jnp.where(key <= place, scores, -1e30)
                held[at_k, :] = scores
                return jnp.maximum(top, jnp.max(scores.reshape(bk // 8, 8, bq), 0))

            top = jnp.full((8, bq), -1e30, F32)
            top = lax.fori_loop(0, i * (bq // bk), score, top)
            for d in range(bq // bk):
                top = score(i * (bq // bk) + d, top, True)
            top = jnp.max(top, 0, keepdims=True)

            def weigh(j, carry):
                total, output = carry
                at_k = pl.ds(pl.multiple_of(j * bk, bk), bk)
                weights = jnp.exp(held[at_k, :] - top)
                held[at_k, :] = weights
                total = total + jnp.sum(weights.reshape(bk // 8, 8, bq), 0)
                return total, output + nn(v_turned[:, at_k], weights.astype(BF16))

            total, output = lax.fori_loop(
                0, blocks, weigh, (jnp.zeros((8, bq), F32), jnp.zeros((width, bq), F32))
            )
            inverse = 1.0 / jnp.sum(total, 0, keepdims=True)
            output = output * inverse
            g_turned = g_head.T.astype(F32)
            inner = jnp.sum(output * g_turned, 0, keepdims=True) * inverse
            g_scaled = (g_turned * inverse).astype(BF16)
            g_rows = g_scaled.T

            def back(j, total):
                at_k = pl.ds(pl.multiple_of(j * bk, bk), bk)
                weights = held[at_k, :]
                prob_grad = nn(v_all[at_k, :], g_scaled)
                score_grad = (weights * (prob_grad - inner)).astype(BF16)
                dv_all[at_k, :] += nn(weights.astype(BF16), g_rows)
                dk_all[at_k, :] += nn(score_grad, q_head)
                return total + nn(k_turned[:, at_k], score_grad)

            q_grad = lax.fori_loop(0, blocks, back, jnp.zeros((width, bq), F32)) * scale
            outs_now = jnp.where(row_head == h, output, outs_now)
            grads_now = jnp.where(row_head == h, q_grad, grads_now)
        o_all[at_q, :] = outs_now.T.astype(BF16)
        dq_all[at_q, :] = grads_now.T.astype(BF16)
        return 0

    lax.fori_loop(0, length // bq, one_block, 0)
    for m in range(parts):
        at = pl.ds(pl.multiple_of((me ^ m) * rows, rows), rows)
        out, i = (outs[m], 0) if len(outs) == parts else (outs[min(m, 2)], max(m - 2, 0))
        out[i, 0] = o_all[at, :]
        out[i, 1] = dq_all[at, :]
        out[i, 2] = dk_all[at, :].astype(BF16)
        out[i, 3] = dv_all[at, :].astype(BF16)


def attend(context, pieces, paired):
    parts = len(pieces)
    seqs, _, rows, width = pieces[0].shape
    length = rows * parts
    bq = min(1024, length)
    bk = bq
    vmem = pltpu.VMEM
    counts = [1, 1, 2] if paired else [seqs] * parts
    return pl.pallas_call(
        functools.partial(attend_kernel, parts, bq, bk),
        out_shape=[jax.ShapeDtypeStruct((n, 4, rows, width), BF16) for n in counts],
        grid_spec=pltpu.PrefetchScalarGridSpec(
            num_scalar_prefetch=1,
            grid=(seqs,),
            in_specs=[pl.BlockSpec((1, 4, rows, width), lambda s, me: (s, 0, 0, 0))] * parts,
            out_specs=[
                pl.BlockSpec((n if paired else 1, 4, rows, width), lambda s, me: (s, 0, 0, 0))
                for n in counts
            ],
            scratch_shapes=[vmem((length, width), BF16)] * 4
            + [vmem((width, length), BF16)] * 2
            + [vmem((length, width), BF16)] * 2
            + [vmem((length, width), F32)] * 2
            + [vmem((length, bq), F32)],
        ),
        compiler_params=pltpu.CompilerParams(vmem_limit_bytes=VMEM_BYTES),
        cost_estimate=lasting(28),
        name="attend",
    )(context, *pieces)


def unturn_kernel(parts, c_ref, *refs):
    pieces = refs[:parts]
    cosine, below, above = refs[parts : parts + 3]
    merged, raw, sums = refs[-3:]
    width = merged.shape[1]
    span = width // parts
    for m in range(parts):
        at = pl.ds(pl.multiple_of((m ^ c_ref[0]) * span, span), span) if parts > 1 else slice(None)
        merged[:, at] = pieces[m][0, 0]
    for c in range(3):
        for m in range(parts):
            for lane in range(0, span, LANES):
                start = (m ^ c_ref[0]) * span + c * width + lane if parts > 1 else c * width + lane
                at = pl.ds(pl.multiple_of(start, LANES), LANES)
                part = pieces[m][0, c + 1, :, lane : lane + LANES]
                if c < 2:
                    part = turn(part.astype(F32), cosine[...], -below[...], -above[...])
                    part = part.astype(BF16)
                raw[:, at] = part
                sums[:, at] = jnp.sum(part.astype(F32), 0, keepdims=True)


def unturn(context, pieces, tables, s, rows, earlier):
    parts = len(pieces)
    length, span = pieces[0].shape[2:]
    width = span * parts
    vmem = pl.BlockSpec(memory_space=pltpu.VMEM)
    return pl.pallas_call(
        functools.partial(unturn_kernel, parts),
        out_shape=[
            jax.ShapeDtypeStruct((rows, width), BF16),
            jax.ShapeDtypeStruct((rows, 3 * width), BF16),
            jax.ShapeDtypeStruct((1, 3 * width), F32),
        ],
        grid=(1,),
        in_specs=[pl.BlockSpec(memory_space=pltpu.SMEM)]
        + [vmem] * (parts + 3)
        + [pl.BlockSpec(memory_space=pl.ANY)] * len(earlier),
        out_specs=[
            pl.BlockSpec((length, width), lambda i: (s, 0)),
            pl.BlockSpec((length, 3 * width), lambda i: (s, 0)),
            vmem,
        ],
        input_output_aliases={parts + 4 + i: i for i in range(len(earlier))},
        compiler_params=pltpu.CompilerParams(vmem_limit_bytes=VMEM_BYTES),
        cost_estimate=lasting(4),
        name="unturn",
    )(context, *pieces, *tables, *earlier)


def norm_back_kernel(count, k_ref, raw, back, *refs):
    width = refs[0].shape[2]
    total = back[...].astype(F32)
    for c in range(3):
        weight = jnp.concatenate([w[c] for w in refs[:count]], 0)
        total = total + nt(raw[:, c * width : (c + 1) * width], weight)
    refs[-1][...] = total.astype(BF16)


def norm_back(place, raw, back, own, rest, s, seqs, earlier):
    rows, depth = back.shape
    width = own.shape[2]
    block = rest[0].shape[1]
    count = own.shape[1] // block
    length = rows // seqs
    tile = min(256, length)
    skip = s * (length // tile)

    def own_spec(p):
        return pl.BlockSpec((3, block, width), lambda r, k: (0, p ^ k[0], 0))

    specs = [own_spec(p) for p in range(count)] + [
        pl.BlockSpec((3, block, width), lambda r, k: (0, 0, 0))
    ] * len(rest)
    some = pl.BlockSpec((tile, depth), lambda r, k: (r + skip, 0))
    return pl.pallas_call(
        functools.partial(norm_back_kernel, len(specs)),
        out_shape=jax.ShapeDtypeStruct((rows, depth), BF16),
        grid_spec=pltpu.PrefetchScalarGridSpec(
            num_scalar_prefetch=1,
            grid=(length // tile,),
            in_specs=[pl.BlockSpec((tile, 3 * width), lambda r, k: (r + skip, 0)), some]
            + specs
            + [pl.BlockSpec(memory_space=pl.ANY)] * len(earlier),
            out_specs=some,
        ),
        input_output_aliases={3 + len(specs) + i: i for i in range(len(earlier))},
        compiler_params=pltpu.CompilerParams(vmem_limit_bytes=VMEM_BYTES),
        cost_estimate=lasting(8),
        name="norm_back",
    )(place, raw, back, *([own] * count), *rest, *earlier)


def gelu_pair(value):
    square = value * value
    bent = jnp.tanh(ROOT * value * (1.0 + CUBE * square))
    half = 0.5 * (1.0 + bent)
    slope = half + 0.5 * value * (1.0 - bent * bent) * (ROOT * (1.0 + 3.0 * CUBE * square))
    return value * half, slope


def feed_kernel(first_count, second_count, onto, k_ref, *refs):
    normed, grad, bias = refs[:3]
    ends = (3 + first_count, 3 + first_count + second_count)
    first = jnp.concatenate([r[...] for r in refs[3 : ends[0]]], 0)
    second = jnp.concatenate([r[...] for r in refs[ends[0] : ends[1]]], 1)
    hidden_out, pre_grad_out, sum_out, fed_out, back_out, fed, back = refs[ends[1] + onto :]
    tile = pl.program_id(0)

    @pl.when(tile == 0)
    def _():
        if onto:
            fed[...] = refs[ends[1]][...].astype(F32)
            back[...] = refs[ends[1] + 1][...].astype(F32)
        else:
            fed[...] = jnp.zeros_like(fed)
            back[...] = jnp.zeros_like(back)

    hidden, slope = gelu_pair(nn(normed[...], first) + bias[...])
    hidden_low = hidden.astype(BF16)
    pre_grad = (nt(grad[...], second) * slope).astype(BF16)
    hidden_out[...] = hidden_low
    pre_grad_out[...] = pre_grad
    fed[...] += nn(hidden_low, second)
    back[...] += nt(pre_grad, first)
    sum_out[...] = jnp.sum(pre_grad.astype(F32), 0, keepdims=True)

    @pl.when(tile == pl.num_programs(0) - 1)
    def _():
        fed_out[...] = fed[...].astype(BF16)
        back_out[...] = back[...].astype(BF16)


def feed(
    place, block, normed, grad, bias, own_first, rest_first, own_second, rest_second, part, sums
):
    rows, width = normed.shape
    inside = rest_first[0].shape[0] // block
    units = rest_first[0].shape[1]
    count = own_first.shape[0] // block
    tile = min(512, units)
    skip = part * (units // tile)
    whole = pl.BlockSpec((rows, width), lambda t, k: (0, 0), pipeline_mode=pl.Buffered(1))

    def first_spec(p):
        return pl.BlockSpec((block, tile), lambda t, k: (p ^ k[0], t + skip))

    def second_spec(p):
        return pl.BlockSpec((tile, block), lambda t, k: (t + skip, p ^ k[0]))

    def first_rest(p):
        return pl.BlockSpec((block, tile), lambda t, k: (p ^ (k[0] % inside), t))

    def second_rest(p):
        return pl.BlockSpec((tile, block), lambda t, k: (t, p ^ (k[0] % inside)))

    first = [first_spec(p) for p in range(count)]
    first += [first_rest(p) for p in range(inside)] * len(rest_first)
    second = [second_spec(p) for p in range(count)]
    second += [second_rest(p) for p in range(inside)] * len(rest_second)
    unit_rows = pl.BlockSpec((rows, tile), lambda t, k: (0, t))
    return pl.pallas_call(
        functools.partial(feed_kernel, len(first), len(second), len(sums)),
        out_shape=[
            jax.ShapeDtypeStruct((rows, units), BF16),
            jax.ShapeDtypeStruct((rows, units), BF16),
            jax.ShapeDtypeStruct((1, units), F32),
            jax.ShapeDtypeStruct((rows, width), BF16),
            jax.ShapeDtypeStruct((rows, width), BF16),
        ],
        grid_spec=pltpu.PrefetchScalarGridSpec(
            num_scalar_prefetch=1,
            grid=(units // tile,),
            in_specs=[whole, whole, pl.BlockSpec((1, tile), lambda t, k: (0, t + skip))]
            + first
            + second
            + [whole] * len(sums),
            out_specs=[
                unit_rows,
                unit_rows,
                pl.BlockSpec((1, tile), lambda t, k: (0, t)),
                whole,
                whole,
            ],
            scratch_shapes=[pltpu.VMEM((rows, width), F32)] * 2,
        ),
        compiler_params=pltpu.CompilerParams(vmem_limit_bytes=VMEM_BYTES),
        cost_estimate=lasting(31),
        name="feed",
    )(
        place,
        normed,
        grad,
        bias,
        *([own_first] * count),
        *[piece for piece in rest_first for _ in range(inside)],
        *([own_second] * count),
        *[piece for piece in rest_second for _ in range(inside)],
        *sums,
    )


def outer_kernel(steps, adds, *refs):
    count = len(steps)
    lefts, rights = refs[: 2 * count], refs[2 * count : 3 * count]
    outs = refs[3 * count + adds : -1]
    turned = refs[-1]
    quarter = lefts[0].shape[1]
    step = pl.program_id(0)
    start = 0
    for i in range(count):

        @pl.when(step == start)
        def _():
            turned[:quarter, :] = lefts[2 * i][...].T
            turned[quarter:, :] = lefts[2 * i + 1][...].T

        @pl.when((step >= start) & (step < start + steps[i]))
        def _():
            value = nn(turned[...], rights[i][...])
            for high in range(2):
                part = value[high * quarter : (high + 1) * quarter]
                if adds:
                    part = part + refs[3 * count][high].astype(F32)
                    outs[high * count + i][...] = part.astype(BF16)
                else:
                    outs[0][high] = part.astype(BF16)

        start += steps[i]


def outer(order, pairs, low, received):
    rows, width = pairs[0][0].shape
    quarter = width // 4
    tile = min([512] + [right.shape[1] for _, right in pairs])
    steps = [right.shape[1] // tile for _, right in pairs]
    total = sum(steps) * tile
    adds = received is not None

    def left_spec(high):
        return pl.BlockSpec((rows, quarter), lambda t: (0, 2 * high + low))

    def column_spec(height, i):
        start = sum(steps[:i])
        return pl.BlockSpec((height, tile), lambda t: (0, jnp.clip(t - start, 0, steps[i] - 1)))

    both = pl.BlockSpec((2, quarter, tile), lambda t: (0, 0, t))
    if adds:
        out_shape = [
            jax.ShapeDtypeStruct((quarter, right.shape[1]), BF16) for _, right in pairs
        ] * 2
        out_specs = [column_spec(quarter, i) for i in range(len(pairs))] * 2
    else:
        out_shape = [jax.ShapeDtypeStruct((2, quarter, total), BF16)]
        out_specs = [both]
    results = pl.pallas_call(
        functools.partial(outer_kernel, steps, int(adds)),
        out_shape=out_shape,
        grid=(sum(steps),),
        in_specs=[left_spec(high) for _ in pairs for high in range(2)]
        + [column_spec(rows, i) for i in range(len(pairs))]
        + [both] * adds,
        out_specs=out_specs,
        scratch_shapes=[pltpu.VMEM((2 * quarter, rows), BF16)],
        compiler_params=pltpu.CompilerParams(vmem_limit_bytes=VMEM_BYTES),
        cost_estimate=lasting(11),
        name="outer",
    )(
        *[left for left, _ in pairs for _ in range(2)],
        *[order(right) if i == 0 else right for i, (_, right) in enumerate(pairs)],
        *([received] if adds else []),
    )
    order.mark(results[0])
    return results


def add_turned_kernel(left, right, out):
    out[...] = add_low(left[...], right[...])


def add_turned(left, right, mask, block):
    rows, width = left.shape
    tile = width
    spec = pl.BlockSpec((block, tile), lambda p, t: (p, t))
    return pl.pallas_call(
        add_turned_kernel,
        out_shape=jax.ShapeDtypeStruct((rows, width), BF16),
        grid=(rows // block, width // tile),
        in_specs=[spec, pl.BlockSpec((block, tile), lambda p, t: (p ^ mask, t))],
        out_specs=spec,
        cost_estimate=lasting(2.5),
        name="add_turned",
    )(left, right)


def finish_kernel(half, tiles, turned, k_ref, *refs):
    out = refs[-1]
    for i, piece in enumerate(refs[:-1]):
        here = pl.program_id(0) // half == i % 2
        if tiles is not None:
            here = here & (pl.program_id(1) // tiles == i // 2)

        @pl.when(here)
        def _():
            value = piece[...].astype(F32)
            value = value.T if turned else value
            out[...] = value.reshape(out.shape)


def finish(place, parts, block, turned=False, groups=1):
    rows, some = parts[0][0].shape
    width = some * len(parts)
    half = rows // block
    if groups > 1:
        tile = width // groups
        shape = (groups, 2 * rows, tile)
        out_spec = pl.BlockSpec((1, block, tile), lambda p, t, k: (t, p ^ k[0], 0))
    elif turned:
        tile = min(1024, some)
        shape = (width, 2 * rows)
        out_spec = pl.BlockSpec((tile, block), lambda p, t, k: (t, p ^ k[0]))
    else:
        tile = min(1024, some)
        shape = (2 * rows, width)
        out_spec = pl.BlockSpec((block, tile), lambda p, t, k: (p ^ k[0], t))
    tiles = some // tile

    def piece_spec(part, side):
        def index(p, t, k):
            return (
                jnp.clip(p - side * half, 0, half - 1),
                jnp.clip(t - part * tiles, 0, tiles - 1),
            )

        return pl.BlockSpec((block, tile), index)

    return pl.pallas_call(
        functools.partial(finish_kernel, half, tiles if len(parts) > 1 else None, turned),
        out_shape=jax.ShapeDtypeStruct(shape, F32),
        grid_spec=pltpu.PrefetchScalarGridSpec(
            num_scalar_prefetch=1,
            grid=(2 * half, width // tile),
            in_specs=[piece_spec(part, side) for part in range(len(parts)) for side in (0, 1)],
            out_specs=out_spec,
        ),
        compiler_params=pltpu.CompilerParams(vmem_limit_bytes=VMEM_BYTES),
        cost_estimate=lasting(8),
        name="finish",
    )(place, *[piece for part in parts for piece in part])


def rotation_tables(positions):
    half = ROT // 2
    exponents = lax.iota(jnp.int32, half).astype(F32) * (2.0 / ROT)
    angles = positions[:, None] * jnp.power(10000.0, -exponents)[None, :]
    cosine, sine = jnp.cos(angles), jnp.sin(angles)
    ones = jnp.ones((positions.shape[0], HD - ROT), F32)
    none = jnp.zeros_like(ones)
    nought = jnp.zeros_like(sine)
    copies = LANES // HD
    return (
        jnp.concatenate([cosine, cosine, ones] * copies, 1),
        jnp.concatenate([-sine, nought, none] * copies, 1),
        jnp.concatenate([nought, sine, none] * copies, 1),
    )


def per_device(
    tokens, ln_gain, ln_bias, w_qkv, b_qkv, w_out, b_out, w_fc1, b_fc1, w_fc2, b_fc2, cotangent
):
    seqs, length, width = tokens.shape
    size = lax.axis_size("context")
    context = lax.axis_index("context")
    shard = lax.axis_index("fsdp")
    tensor_size = lax.axis_size("tensor")
    tensor = lax.axis_index("tensor")
    across = size // 2
    place = (context & 1) * across + context // 2
    me = shard * size + place
    block = width // (2 * size)
    rows = seqs * length
    heads_width = w_out.shape[0]
    heads_local = heads_width // HD
    head_groups = min(heads_local, size)
    seq_groups = size // head_groups
    span = heads_width // head_groups
    direct = seq_groups == 1 and span % LANES == 0 and size == 4
    me_s, place_s, context_s = (jnp.reshape(v, (1,)).astype(jnp.int32) for v in (me, place, context))

    small = (ln_gain, ln_bias, b_out, b_fc2, b_fc1, b_qkv.reshape(-1))
    packed = jnp.concatenate(small)
    other = to_fsdp(packed)
    halves = 2
    units = w_fc1.shape[1] // halves

    def qkv_at(p):
        return lax.dynamic_slice_in_dim(w_qkv, (place ^ p) * block, block, 1)

    def out_at(p):
        return lax.dynamic_slice_in_dim(w_out, (place ^ p) * block, block, 1)

    flat = tokens.reshape(rows, width)
    grad_flat = cotangent.reshape(rows, width)
    both = jnp.where(shard == 0, jnp.stack([packed, other]), jnp.stack([other, packed]))
    both = both.astype(F32)
    vectors = []
    at = 0
    for value in small:
        vectors.append(both[:, at : at + value.size])
        at += value.size
    gain, bias, out_bias, fc2_bias, fc1_bias = (v.reshape(1, -1) for v in vectors[:5])
    qkv_bias = jnp.swapaxes(vectors[5].reshape(2, 3, -1), 0, 1).reshape(3, 1, heads_width)
    normed, grad, bias_sum = prepare(me_s, 2 * size, flat, grad_flat, gain, bias)
    positions = (context * length + lax.iota(jnp.int32, length)).astype(F32)
    tables = rotation_tables(positions)
    bias_sum, *tables = lax.optimization_barrier((bias_sum, *tables))

    order = Order()
    half = across * block
    core = context & 1

    def fc_from(i, *done):
        first = lax.dynamic_slice(w_fc1, (core * half, i * units), (half, units))
        second = lax.dynamic_slice(w_fc2, (i * units, core * half), (units, half))
        return to_fsdp(after(first, *done)), to_fsdp(after(second, *done))

    rest_qkv = [to_fsdp(qkv_at(0))]
    ready = rest_qkv[0]
    rest_out = [to_fsdp(after(out_at(0), ready))]

    def first_from(i, *done):
        part = lax.dynamic_slice(w_fc1, (core * half, i * units), (half, units))
        return to_fsdp(after(part, *done))

    def second_from(i, *done):
        part = lax.dynamic_slice(w_fc2, (i * units, core * half), (units, half))
        return to_fsdp(after(part, *done))

    first_near = [first_from(0, ready)]
    order.mark(bias_sum)
    for mask in masks_of(across):
        rest_qkv = rest_qkv + [to_context(piece, 2 * mask) for piece in rest_qkv]
    waited = order.wait(*rest_qkv, *rest_out)
    rest_qkv, rest_out = list(waited[: len(rest_qkv)]), list(waited[len(rest_qkv) :])
    for mask in masks_of(across):
        rest_out = rest_out + [to_context(piece, 2 * mask) for piece in rest_out]
    rest_qkv = rest_qkv + [to_context(piece, 1) for piece in rest_qkv]
    waited = order.wait(first_near[0], *rest_out)
    first_near[0], rest_out = waited[0], list(waited[1:])
    second_near = [second_from(0, first_near[0])]
    rest_out = rest_out + [to_context(piece, 1) for piece in rest_out]

    near = jnp.concatenate([out_at(p) for p in range(across)] + rest_out[:across], 1)
    near = lax.all_gather(near, "tensor", axis=0, tiled=True)

    pieces = project(
        place_s,
        context_s,
        order(normed),
        grad,
        w_qkv,
        rest_qkv,
        w_out,
        rest_out,
        qkv_bias,
        tables,
        seqs,
        size if direct else 1,
    )
    def send_across(own, beside, across_pair):
        return own, beside, to_context(across_pair, 2)

    def pass_on(own, beside, far_pair):
        (far_pair,) = order.wait(far_pair)
        return [own, to_context(order(beside), 1), far_pair[:1], to_context(far_pair[1:], 1)]

    if direct:
        here = [send_across(*pieces[0])]
    else:
        field = jnp.concatenate([row[0] for row in pieces], 0)

        def part_for(mask):
            target = context ^ mask
            starts = [0] * 4
            sizes = list(field.shape)
            starts[0] = (target // head_groups) * (seqs // seq_groups)
            sizes[0] = seqs // seq_groups
            starts[3] = (target % head_groups) * span
            sizes[3] = span
            return lax.dynamic_slice(field, starts, sizes)

        here = [[part_for(0)] + [to_context(part_for(m), m) for m in range(1, size)]]

    order.mark(pieces[0][0])

    sums = ()
    fed_parts = []
    back = []

    def feed_part(i, sums):
        first, second = first_near[i], second_near[i]
        hidden, pre_grad, pre_sum, *sums = feed(
            place_s,
            block,
            order(normed),
            grad,
            fc1_bias,
            w_fc1,
            [first, to_context(first, 1)],
            w_fc2,
            [second, to_context(second, 1)],
            i,
            tuple(sums),
        )
        fed_parts.append((hidden, pre_grad, order.mark(pre_sum)))
        return sums

    rows_here = list(here)
    for i in range(max(halves, len(pieces) if direct else 1)):
        if i < halves:
            (second_near[i],) = order.wait(second_near[i])
            if i + 1 < halves:
                first_near.append(first_from(i + 1, second_near[i]))
            sums = feed_part(i, sums)
            if i + 1 < halves:
                (first_near[i + 1],) = order.wait(first_near[i + 1])
                second_near.append(second_from(i + 1, first_near[i + 1]))
        if i == halves - 1:
            fed, fed_back = sums
            fed_share = lax.psum_scatter(fed, "tensor", scatter_dimension=0, tiled=True)
            fc_sums = [
                Reduction(order, ((normed, part[1]), (grad, part[0])), block)
                for part in fed_parts
            ]
            fc_sums[0].send()
        if i < len(here):
            if direct and i == 0:
                rows_here = [pass_on(*here[0])]
                for own, beside, across_pair in pieces[1:]:
                    across_pair = after(order(across_pair), here[-1][2])
                    here.append(send_across(own, beside, across_pair))
            row = rows_here[i]
            result = attend(context_s, [order(row[0])] + row[1:], direct)
            order.mark(result[0])
            if direct:
                back.append(send_across(*result))
                if i + 1 < len(here):
                    rows_here.append(pass_on(*here[i + 1]))
            else:
                back.append(
                    [result[0]] + [to_context(result[m], m) for m in range(1, size)]
                )
    if not direct:
        stacked = jnp.stack(back[0])
        sources = lax.iota(jnp.int32, size) ^ context
        ordered = jnp.take(stacked, sources, axis=0)
        ordered = ordered.reshape(seq_groups, head_groups, seqs // seq_groups, 4, length, span)
        ordered = jnp.transpose(ordered, (0, 2, 3, 4, 1, 5))
        ordered = ordered.reshape(seqs, 4, length, heads_width)
        back = [[ordered[s : s + 1]] for s in range(seqs)]

    def through(s, unturned, norm_terms):
        row = [order(back[s][0])] + back[s][1:]
        *unturned, part_sum = unturn(context_s, row, tables, s, rows, tuple(unturned))
        norm_terms = norm_back(
            place_s, unturned[1], fed_back, w_qkv, rest_qkv, s, seqs, tuple(norm_terms)
        )
        order.mark(norm_terms)
        return unturned, [norm_terms], part_sum

    first_sum, second_sum = fc_sums
    if direct:
        back[0] = pass_on(*back[0])
    first_sum.keep()
    first_sum.over_fsdp(0)
    unturned = []
    norm_terms = ()
    qkv_bias_sum = 0.0
    for s in range(seqs):
        if direct and s:
            back[s] = pass_on(*back[s])
        unturned, norm_terms, part_sum = through(s, unturned, norm_terms)
        qkv_bias_sum = qkv_bias_sum + part_sum
    merged, raw_grad = unturned
    norm_share = lax.psum_scatter(norm_terms[0], "tensor", scatter_dimension=0, tiled=True)
    share = rows // tensor_size

    def rows_for(mask):
        return lax.dynamic_slice_in_dim(merged, (tensor ^ mask) * share, share, 0)

    def arrived(*values):
        return order.wait(*values)

    heads_from = [rows_for(0)] + [to_tensor(rows_for(m), m) for m in range(1, tensor_size)]
    last_sum = Reduction(order, ((grad, merged), (normed, raw_grad)), block)
    (first_sum.far[0],) = arrived(first_sum.far[0])
    first_sum.over_fsdp(1, first_sum.far[0])
    first_sum.over_chips(0)
    second_sum.send()
    far = to_context(order(near), 1)
    heads_from[1:] = arrived(*heads_from[1:])

    def in_order(blocks):
        return jnp.concatenate(own_blocks(blocks, 1, me, block), 1).astype(F32)

    inputs = lax.dynamic_slice_in_dim(flat, tensor * share, share, 0).astype(F32)
    all_heads = jnp.zeros((share, tensor_size * heads_width), BF16)
    for m in range(tensor_size):
        all_heads = lax.dynamic_update_slice_in_dim(
            all_heads, order(heads_from[m]), (tensor ^ m) * heads_width, 1
        )
    near_part, far_part = nn(all_heads, near), nn(all_heads, far)
    attended = [near_part[:, :half], far_part[:, :half], near_part[:, half:], far_part[:, half:]]
    branch_sum = in_order(jnp.concatenate(attended, 1) + fed_share.astype(F32))
    block_out = (inputs + branch_sum + out_bias + fc2_bias).astype(BF16)
    order.mark(block_out)
    block_out = lax.all_gather(block_out, "tensor", axis=0, tiled=True).reshape(tokens.shape)
    second_sum.keep()
    first_sum.far[1], first_sum.far[0] = arrived(first_sum.far[1], first_sum.far[0])
    second_sum.over_fsdp(0, first_sum.far[1])
    first_sum.over_chips(1)
    first_sum.over_cores(0)

    normed_grad = in_order(order(norm_share))
    centered = inputs - jnp.mean(inputs, -1, keepdims=True)
    root = lax.rsqrt(jnp.mean(centered * centered, -1, keepdims=True) + EPSILON)
    unit = centered * root
    scaled = normed_grad * gain
    inner = jnp.mean(scaled * unit, -1, keepdims=True)
    input_part = root * (scaled - jnp.mean(scaled, -1, keepdims=True) - unit * inner)
    grad_share = lax.dynamic_slice_in_dim(grad_flat, tensor * share, share, 0).astype(F32)
    tokens_grad = (grad_share + input_part).astype(BF16)
    norm_sums = jnp.stack([jnp.sum(normed_grad * unit, 0), jnp.sum(normed_grad, 0)])
    order.mark(norm_sums)
    order.mark(tokens_grad)
    tokens_grad = lax.all_gather(tokens_grad, "tensor", axis=0, tiled=True).reshape(tokens.shape)

    second_sum.far[0], first_sum.far[1] = arrived(second_sum.far[0], first_sum.far[1])
    second_sum.over_fsdp(1, second_sum.far[0])
    second_sum.over_chips(0)
    last_sum.send()
    first_sum.over_cores(1)
    last_sum.keep()
    second_sum.far[1], second_sum.far[0] = arrived(second_sum.far[1], second_sum.far[0])
    last_sum.over_fsdp(1, second_sum.far[1])
    second_sum.over_chips(1)
    second_sum.over_cores(0)
    fc1_grad = order.mark(
        finish(place_s, [first_sum.pieces[0], second_sum.pieces[0]], block)
    )
    last_sum.far[1], second_sum.far[1] = arrived(last_sum.far[1], second_sum.far[1])
    last_sum.over_fsdp(0, last_sum.far[1])
    last_sum.over_chips(1)
    second_sum.over_cores(1)
    fc2_grad = order.mark(
        finish(place_s, [first_sum.pieces[1], second_sum.pieces[1]], block, turned=True)
    )
    (last_sum.far[0],) = arrived(last_sum.far[0])
    last_sum.over_chips(0)
    last_sum.over_cores(1)
    qkv_grad = order.mark(finish(place_s, [last_sum.pieces[1]], block, groups=3))
    last_sum.over_cores(0)
    out_grad = order.mark(finish(place_s, [last_sum.pieces[0]], block, turned=True))

    units_here = b_fc1.shape[0] * 2
    small_sums = [norm_sums.reshape(1, -1), bias_sum] + [part[2] for part in fed_parts]
    small_sums = jnp.concatenate(small_sums + [qkv_bias_sum], 1)
    small_sums = sum_everywhere(after(small_sums, fc1_grad), False)[0]
    norm_sums = small_sums[: 2 * width].reshape(2, width)
    for mask in masks_of(tensor_size):
        norm_sums = norm_sums + to_tensor(norm_sums, mask)
    other_sums = small_sums[2 * width :]

    def shard_of(value):
        part = value.shape[-1] // 2
        return lax.dynamic_slice_in_dim(value, shard * part, part, value.ndim - 1)

    out_bias_grad = shard_of(other_sums[:width])
    fc1_bias_grad = shard_of(other_sums[width : width + units_here])
    qkv_bias_grad = shard_of(other_sums[width + units_here :].reshape(3, heads_width))
    return (
        block_out,
        tokens_grad,
        shard_of(norm_sums[0]),
        shard_of(norm_sums[1]),
        qkv_grad,
        qkv_bias_grad,
        out_grad,
        out_bias_grad,
        fc1_grad,
        fc1_bias_grad,
        fc2_grad,
        out_bias_grad,
    )


def solution(mesh):
    return jax.shard_map(
        per_device,
        mesh=mesh,
        in_specs=(
            P("fsdp", "context", None),
            P("fsdp"),
            P("fsdp"),
            P(None, "fsdp", "tensor"),
            P(None, ("tensor", "fsdp")),
            P("tensor", "fsdp"),
            P("fsdp"),
            P("fsdp", "tensor"),
            P(("tensor", "fsdp")),
            P("tensor", "fsdp"),
            P("fsdp"),
            P("fsdp", "context", None),
        ),
        out_specs=(
            P("fsdp", "context", None),
            P("fsdp", "context", None),
            P("fsdp"),
            P("fsdp"),
            P(None, "fsdp", "tensor"),
            P(None, ("tensor", "fsdp")),
            P("tensor", "fsdp"),
            P("fsdp"),
            P("fsdp", "tensor"),
            P(("tensor", "fsdp")),
            P("tensor", "fsdp"),
            P("fsdp"),
        ),
        check_vma=False,
    )
```

```python
import functools

import jax
import jax.numpy as jnp
from jax import lax
import jax.experimental.pallas as pl
import jax.experimental.pallas.tpu as pltpu
from jax.sharding import PartitionSpec as P

HD = 64
ROT = 32
EPSILON = 1e-05
LANES = 128
F32 = jnp.float32
BF16 = jnp.bfloat16
ROOT = 0.7978845608028654
CUBE = 0.044715
VMEM_BYTES = 60 << 20


def lasting(micros):
    return pl.CostEstimate(flops=0, bytes_accessed=int(micros * 3.4e6), transcendentals=0)


def nn(a, b):
    return lax.dot_general(a, b, (((1,), (0,)), ((), ())), preferred_element_type=F32)


def nt(a, b):
    return lax.dot_general(a, b, (((1,), (1,)), ((), ())), preferred_element_type=F32)


def tn(a, b):
    return lax.dot_general(a, b, (((0,), (0,)), ((), ())), preferred_element_type=F32)


def add_low(*terms):
    total = terms[0].astype(F32)
    for term in terms[1:]:
        total = total + term.astype(F32)
    return total.astype(BF16)


def to_fsdp(value):
    return lax.ppermute(value, "fsdp", [(0, 1), (1, 0)])


def to_context(value, mask):
    size = lax.axis_size("context")
    return lax.ppermute(value, "context", [(i, i ^ mask) for i in range(size)])


def to_tensor(value, mask):
    size = lax.axis_size("tensor")
    return lax.ppermute(value, "tensor", [(i, i ^ mask) for i in range(size)])


def after(value, *others):
    return lax.optimization_barrier((value,) + others)[0]


def masks_of(size):
    mask = 1
    while mask < size:
        yield mask
        mask *= 2


def own_blocks(own, axis, place, block):
    count = own.shape[axis] // block
    return [
        lax.dynamic_slice_in_dim(own, (p ^ place) * block, block, axis) for p in range(count)
    ]


class Order:
    def __init__(self):
        self.last = None

    def __call__(self, value):
        return value if self.last is None else after(value, self.last)

    def mark(self, value):
        self.last = value
        return value

    def wait(self, *values):
        if self.last is not None:
            values = lax.optimization_barrier(values + (self.last,))[:-1]
        else:
            values = lax.optimization_barrier(values)
        self.last = values[0]
        return values


class Reduction:
    def __init__(self, order, pairs, block):
        self.order, self.pairs, self.block = order, pairs, block

    def send(self):
        (self.sent,) = outer(self.order, self.pairs, 1, None)
        self.sent = to_context(self.sent, 1)

    def keep(self):
        results = outer(self.order, self.pairs, 0, self.sent)
        self.near, self.far = results[: len(self.pairs)], results[len(self.pairs) :]
        self.near, self.far = list(self.near), list(self.far)
        self.pieces = [None] * len(self.pairs)

    def over_fsdp(self, i, *earlier):
        self.far[i] = to_fsdp(after(self.far[i], *earlier) if earlier else self.far[i])
        return self.far[i]

    def over_chips(self, i):
        self.near[i] = self.order.mark(add_low(self.order(self.near[i]), self.far[i]))
        self.masks = list(masks_of(lax.axis_size("context") // 2))
        if self.masks:
            self.far[i] = to_context(self.near[i], 2 * self.masks[0])
        return self.far[i]

    def over_cores(self, i):
        total = self.near[i]
        for n, mask in enumerate(self.masks):
            other = self.far[i] if n == 0 else to_context(total, 2 * mask)
            total = self.order.mark(add_turned(self.order(total), other, mask, self.block))
        self.pieces[i] = (total, to_context(total, 1))


def prepare_kernel(count, me_ref, tokens, grad, gain, bias, normed_out, grad_out, sum_out, kept):
    values = tokens[...].astype(F32)
    centered = values - jnp.mean(values, -1, keepdims=True)
    variance = jnp.mean(centered * centered, -1, keepdims=True)
    kept[...] = (centered * lax.rsqrt(variance + EPSILON) * gain[...] + bias[...]).astype(BF16)
    me = me_ref[0]
    block = tokens.shape[1] // count
    for p in range(count):
        source = pl.ds(pl.multiple_of((p ^ me) * block, block), block)
        normed_out[:, p * block : (p + 1) * block] = kept[:, source]
        grad_out[:, p * block : (p + 1) * block] = grad[:, source]
    part = jnp.sum(grad[...].astype(F32), 0, keepdims=True)

    @pl.when(pl.program_id(0) == 0)
    def _():
        sum_out[...] = part

    @pl.when(pl.program_id(0) > 0)
    def _():
        sum_out[...] += part


def prepare(me, count, tokens, grad, gain, bias):
    rows, width = tokens.shape
    tile = min(128, rows)
    row_spec = pl.BlockSpec((tile, width), lambda r, me: (r, 0))
    one_spec = pl.BlockSpec((1, width), lambda r, me: (0, 0))
    return pl.pallas_call(
        functools.partial(prepare_kernel, count),
        out_shape=[
            jax.ShapeDtypeStruct((rows, width), BF16),
            jax.ShapeDtypeStruct((rows, width), BF16),
            jax.ShapeDtypeStruct((1, width), F32),
        ],
        grid_spec=pltpu.PrefetchScalarGridSpec(
            num_scalar_prefetch=1,
            grid=(rows // tile,),
            in_specs=[row_spec, row_spec, one_spec, one_spec],
            out_specs=[row_spec, row_spec, one_spec],
            scratch_shapes=[pltpu.VMEM((tile, width), BF16)],
        ),
        compiler_params=pltpu.CompilerParams(vmem_limit_bytes=VMEM_BYTES),
        cost_estimate=lasting(10),
        name="prepare",
    )(me, tokens, grad, gain, bias)


def turn(part, cosine, below, above):
    return (
        part * cosine
        + pltpu.roll(part, LANES - ROT // 2, 1) * below
        + pltpu.roll(part, ROT // 2, 1) * above
    )


def project_kernel(seqs, qkv_count, out_count, parts, k_ref, c_ref, *refs):
    normed, grad, bias, cosine, below, above = refs[:6]
    ends = (6 + qkv_count, 6 + qkv_count + out_count)
    outs, kept = refs[ends[1] : -1], refs[-1]
    which = pl.program_id(0)
    rows, width = kept.shape
    length = rows // seqs

    @pl.when(which < 3)
    def _():
        weight = jnp.concatenate([w[0] for w in refs[6 : ends[0]]], 0)
        raw = nn(normed[...], weight) + bias[0]

        @pl.when(which < 2)
        def _():
            for s in range(seqs):
                for lane in range(0, width, LANES):
                    part = raw[s * length : (s + 1) * length, lane : lane + LANES]
                    kept[s * length : (s + 1) * length, lane : lane + LANES] = turn(
                        part, cosine[...], below[...], above[...]
                    ).astype(BF16)

        @pl.when(which == 2)
        def _():
            kept[...] = raw.astype(BF16)

    @pl.when(which == 3)
    def _():
        weight = jnp.concatenate([w[...] for w in refs[ends[0] : ends[1]]], 1)
        kept[...] = nt(grad[...], weight).astype(BF16)

    span = width // parts
    for m in range(parts):
        at = pl.ds(pl.multiple_of((m ^ c_ref[0]) * span, span), span) if parts > 1 else slice(None)
        for s in range(seqs):
            part = kept[s * length : (s + 1) * length, at]
            if parts == 1:
                outs[s][0, 0] = part
            else:
                outs[3 * s + min(m, 2)][max(m - 2, 0), 0] = part


def project(place, context, normed, grad, qkv, qkv_rest, out, out_rest, bias, tables, seqs, parts):
    rows, depth = normed.shape
    width = qkv.shape[2]
    block = qkv_rest[0].shape[1]
    count = qkv.shape[1] // block
    length = rows // seqs
    span = width // parts
    table = pl.BlockSpec((length, LANES), lambda c, k, x: (0, 0))
    whole = pl.BlockSpec((rows, depth), lambda c, k, x: (0, 0), pipeline_mode=pl.Buffered(1))

    def qkv_spec(p):
        return pl.BlockSpec((1, block, width), lambda c, k, x: (jnp.minimum(c, 2), p ^ k[0], 0))

    def out_spec(p):
        return pl.BlockSpec((width, block), lambda c, k, x: (0, p ^ k[0]))

    qkv_specs = [qkv_spec(p) for p in range(count)] + [
        pl.BlockSpec((1, block, width), lambda c, k, x: (jnp.minimum(c, 2), 0, 0))
    ] * len(qkv_rest)
    out_specs = [out_spec(p) for p in range(count)] + [
        pl.BlockSpec((width, block), lambda c, k, x: (0, 0))
    ] * len(out_rest)
    counts = [1] if parts == 1 else [1, 1, 2]
    results = pl.pallas_call(
        functools.partial(project_kernel, seqs, len(qkv_specs), len(out_specs), parts),
        out_shape=[jax.ShapeDtypeStruct((n, 4, length, span), BF16) for n in counts] * seqs,
        grid_spec=pltpu.PrefetchScalarGridSpec(
            num_scalar_prefetch=2,
            grid=(4,),
            in_specs=[
                whole,
                whole,
                pl.BlockSpec((1, 1, width), lambda c, k, x: (jnp.minimum(c, 2), 0, 0)),
                table,
                table,
                table,
            ]
            + qkv_specs
            + out_specs,
            out_specs=[
                pl.BlockSpec((n, 1, length, span), lambda c, k, x: (0, c, 0, 0)) for n in counts
            ]
            * seqs,
            scratch_shapes=[pltpu.VMEM((rows, width), BF16)],
        ),
        compiler_params=pltpu.CompilerParams(vmem_limit_bytes=VMEM_BYTES),
        cost_estimate=lasting(19),
        name="project",
    )(
        place,
        context,
        normed,
        grad,
        bias,
        *tables,
        *([qkv] * count),
        *qkv_rest,
        *([out] * count),
        *out_rest,
    )
    return [results[s * len(counts) : (s + 1) * len(counts)] for s in range(seqs)]


def attend_kernel(parts, bq, bk, me_ref, *refs):
    pieces = refs[:parts]
    outs = refs[parts:-11]
    q_all, k_all, v_all, g_all, v_turned, k_turned, o_all, dq_all, dk_all, dv_all, held = refs[-11:]
    rows, width = pieces[0].shape[2:]
    length = rows * parts
    me = me_ref[0]
    scale = HD**-0.5
    for m in range(parts):
        at = pl.ds(pl.multiple_of((me ^ m) * rows, rows), rows)
        q_all[at, :] = (pieces[m][0, 0].astype(F32) * scale).astype(BF16)
        k_all[at, :] = pieces[m][0, 1]
        v_all[at, :] = pieces[m][0, 2]
        g_all[at, :] = pieces[m][0, 3]
    v_turned[...] = v_all[...].T
    k_turned[...] = k_all[...].T
    dk_all[...] = jnp.zeros_like(dk_all)
    dv_all[...] = jnp.zeros_like(dv_all)
    heads = width // HD
    lane_head = lax.broadcasted_iota(jnp.int32, (1, width), 1) // HD

    for first in range(0, length, bq):
        at_q = slice(first, first + bq)
        query, grad = q_all[at_q, :], g_all[at_q, :]
        spans = [slice(k, min(k + bk, first + bq)) for k in range(0, first + bq, bk)]
        outputs, q_grads = [], []
        for h in range(heads):
            at_h = slice(h * HD, (h + 1) * HD)
            q_head = jnp.where(lane_head == h, query, jnp.zeros_like(query))
            g_head = jnp.where(lane_head == h, grad, jnp.zeros_like(grad))
            top = jnp.full((8, bq), -1e30, F32)
            for span in spans:
                scores = nt(k_all[span, :], q_head)
                free = min(span.stop, max(first, span.start)) - span.start
                if free:
                    part = scores[:free]
                    held[span.start : span.start + free, :] = part
                    top = jnp.maximum(top, jnp.max(part.reshape(free // 8, 8, bq), 0))
                rest = span.stop - span.start - free
                if rest:
                    key = span.start + free + lax.broadcasted_iota(jnp.int32, (rest, bq), 0)
                    place = first + lax.broadcasted_iota(jnp.int32, (rest, bq), 1)
                    part = jnp.where(key <= place, scores[free:], -1e30)
                    held[span.start + free : span.stop, :] = part
                    top = jnp.maximum(top, jnp.max(part.reshape(rest // 8, 8, bq), 0))
            top = jnp.max(top, 0, keepdims=True)
            total = jnp.zeros((8, bq), F32)
            output = jnp.zeros((HD, bq), F32)
            for span in spans:
                weights = jnp.exp(held[span, :] - top)
                held[span, :] = weights
                total = total + jnp.sum(weights.reshape(-1, 8, bq), 0)
                output = output + nn(v_turned[at_h, span], weights.astype(BF16))
            inverse = 1.0 / jnp.sum(total, 0, keepdims=True)
            output = output * inverse
            g_turned = g_head.T.astype(F32)
            inner = jnp.sum(output * g_turned[at_h], 0, keepdims=True) * inverse
            g_scaled = (g_turned * inverse).astype(BF16)
            g_rows = g_scaled.T
            q_grad = jnp.zeros((HD, bq), F32)
            for span in spans:
                weights = held[span, :]
                prob_grad = nn(v_all[span, :], g_scaled)
                score_grad = (weights * (prob_grad - inner)).astype(BF16)
                dv_all[span, :] += nn(weights.astype(BF16), g_rows)
                dk_all[span, :] += nn(score_grad, q_head)
                q_grad = q_grad + nn(k_turned[at_h, span], score_grad)
            outputs.append(output)
            q_grads.append(q_grad * scale)
        o_all[at_q, :] = jnp.concatenate(outputs, 0).T.astype(BF16)
        dq_all[at_q, :] = jnp.concatenate(q_grads, 0).T.astype(BF16)
    for m in range(parts):
        at = pl.ds(pl.multiple_of((me ^ m) * rows, rows), rows)
        out, i = (outs[m], 0) if len(outs) == parts else (outs[min(m, 2)], max(m - 2, 0))
        out[i, 0] = o_all[at, :]
        out[i, 1] = dq_all[at, :]
        out[i, 2] = dk_all[at, :].astype(BF16)
        out[i, 3] = dv_all[at, :].astype(BF16)


def attend(context, pieces, paired):
    parts = len(pieces)
    seqs, _, rows, width = pieces[0].shape
    length = rows * parts
    bq = min(512, length)
    bk = min(2048, length)
    vmem = pltpu.VMEM
    counts = [1, 1, 2] if paired else [seqs] * parts
    return pl.pallas_call(
        functools.partial(attend_kernel, parts, bq, bk),
        out_shape=[jax.ShapeDtypeStruct((n, 4, rows, width), BF16) for n in counts],
        grid_spec=pltpu.PrefetchScalarGridSpec(
            num_scalar_prefetch=1,
            grid=(seqs,),
            in_specs=[pl.BlockSpec((1, 4, rows, width), lambda s, me: (s, 0, 0, 0))] * parts,
            out_specs=[
                pl.BlockSpec((n if paired else 1, 4, rows, width), lambda s, me: (s, 0, 0, 0))
                for n in counts
            ],
            scratch_shapes=[vmem((length, width), BF16)] * 4
            + [vmem((width, length), BF16)] * 2
            + [vmem((length, width), BF16)] * 2
            + [vmem((length, width), F32)] * 2
            + [vmem((length, bq), F32)],
        ),
        compiler_params=pltpu.CompilerParams(vmem_limit_bytes=VMEM_BYTES),
        cost_estimate=lasting(28),
        name="attend",
    )(context, *pieces)


def unturn_kernel(parts, c_ref, *refs):
    pieces = refs[:parts]
    cosine, below, above = refs[parts : parts + 3]
    merged, raw, sums = refs[-3:]
    width = merged.shape[1]
    span = width // parts
    for m in range(parts):
        at = pl.ds(pl.multiple_of((m ^ c_ref[0]) * span, span), span) if parts > 1 else slice(None)
        merged[:, at] = pieces[m][0, 0]
    for c in range(3):
        for m in range(parts):
            for lane in range(0, span, LANES):
                start = (m ^ c_ref[0]) * span + c * width + lane if parts > 1 else c * width + lane
                at = pl.ds(pl.multiple_of(start, LANES), LANES)
                part = pieces[m][0, c + 1, :, lane : lane + LANES]
                if c < 2:
                    part = turn(part.astype(F32), cosine[...], -below[...], -above[...])
                    part = part.astype(BF16)
                raw[:, at] = part
                sums[:, at] = jnp.sum(part.astype(F32), 0, keepdims=True)


def unturn(context, pieces, tables, s, rows, earlier):
    parts = len(pieces)
    length, span = pieces[0].shape[2:]
    width = span * parts
    vmem = pl.BlockSpec(memory_space=pltpu.VMEM)
    return pl.pallas_call(
        functools.partial(unturn_kernel, parts),
        out_shape=[
            jax.ShapeDtypeStruct((rows, width), BF16),
            jax.ShapeDtypeStruct((rows, 3 * width), BF16),
            jax.ShapeDtypeStruct((1, 3 * width), F32),
        ],
        grid=(1,),
        in_specs=[pl.BlockSpec(memory_space=pltpu.SMEM)]
        + [vmem] * (parts + 3)
        + [pl.BlockSpec(memory_space=pl.ANY)] * len(earlier),
        out_specs=[
            pl.BlockSpec((length, width), lambda i: (s, 0)),
            pl.BlockSpec((length, 3 * width), lambda i: (s, 0)),
            vmem,
        ],
        input_output_aliases={parts + 4 + i: i for i in range(len(earlier))},
        compiler_params=pltpu.CompilerParams(vmem_limit_bytes=VMEM_BYTES),
        cost_estimate=lasting(4),
        name="unturn",
    )(context, *pieces, *tables, *earlier)


def norm_back_kernel(count, k_ref, raw, back, *refs):
    out, total = refs[-2:]
    weight = jnp.concatenate([w[0] for w in refs[:count]], 0)
    term = nt(raw[...], weight)
    step = pl.program_id(0)

    @pl.when(step == 0)
    def _():
        total[...] = back[...].astype(F32) + term

    @pl.when(step == 1)
    def _():
        total[...] += term

    @pl.when(step == 2)
    def _():
        out[...] = (total[...] + term).astype(BF16).reshape(out.shape)


def norm_back(place, raw, back, own, rest, s, seqs, shares, earlier):
    rows, depth = back.shape
    width = own.shape[2]
    block = rest[0].shape[1]
    count = own.shape[1] // block
    length = rows // seqs

    def own_spec(p):
        return pl.BlockSpec((1, block, width), lambda c, k: (c, p ^ k[0], 0))

    specs = [own_spec(p) for p in range(count)] + [
        pl.BlockSpec((1, block, width), lambda c, k: (c, 0, 0))
    ] * len(rest)
    return pl.pallas_call(
        functools.partial(norm_back_kernel, len(specs)),
        out_shape=jax.ShapeDtypeStruct((shares, seqs, length // shares, depth), BF16),
        grid_spec=pltpu.PrefetchScalarGridSpec(
            num_scalar_prefetch=1,
            grid=(3,),
            in_specs=[
                pl.BlockSpec((length, width), lambda c, k: (s, c)),
                pl.BlockSpec((length, depth), lambda c, k: (s, 0)),
            ]
            + specs
            + [pl.BlockSpec(memory_space=pl.ANY)] * len(earlier),
            out_specs=pl.BlockSpec(
                (shares, 1, length // shares, depth), lambda c, k: (0, s, 0, 0)
            ),
            scratch_shapes=[pltpu.VMEM((length, depth), F32)],
        ),
        input_output_aliases={3 + len(specs) + i: i for i in range(len(earlier))},
        compiler_params=pltpu.CompilerParams(vmem_limit_bytes=VMEM_BYTES),
        cost_estimate=lasting(8),
        name="norm_back",
    )(place, raw, back, *([own] * count), *rest, *earlier)


def gelu_pair(value):
    square = value * value
    bent = jnp.tanh(ROOT * value * (1.0 + CUBE * square))
    half = 0.5 * (1.0 + bent)
    slope = half + 0.5 * value * (1.0 - bent * bent) * (ROOT * (1.0 + 3.0 * CUBE * square))
    return value * half, slope


def feed_kernel(first_count, second_count, onto, seqs, shares, k_ref, *refs):
    normed, grad, bias = refs[:3]
    ends = (3 + first_count, 3 + first_count + second_count)
    first = jnp.concatenate([r[...] for r in refs[3 : ends[0]]], 0)
    second = jnp.concatenate([r[...] for r in refs[ends[0] : ends[1]]], 1)
    hidden_out, pre_grad_out, sum_out, fed_out, back_out, fed, back = refs[ends[1] + onto :]
    tile = pl.program_id(0)

    @pl.when(tile == 0)
    def _():
        if onto:
            fed[...] = refs[ends[1]][...].astype(F32)
            back[...] = refs[ends[1] + 1][...].astype(F32)
        else:
            fed[...] = jnp.zeros_like(fed)
            back[...] = jnp.zeros_like(back)

    hidden, slope = gelu_pair(nn(normed[...], first) + bias[...])
    hidden_low = hidden.astype(BF16)
    pre_grad = (nt(grad[...], second) * slope).astype(BF16)
    hidden_out[...] = hidden_low
    pre_grad_out[...] = pre_grad
    fed[...] += nn(hidden_low, second)
    back[...] += nt(pre_grad, first)
    sum_out[...] = jnp.sum(pre_grad.astype(F32), 0, keepdims=True)

    @pl.when(tile == pl.num_programs(0) - 1)
    def _():
        tile_rows = fed.shape[0] // (seqs * shares)
        for to in range(seqs * shares):
            source = (to % seqs * shares + to // seqs) * tile_rows
            fed_out[to * tile_rows : (to + 1) * tile_rows, :] = fed[
                source : source + tile_rows, :
            ].astype(BF16)
        back_out[...] = back[...].astype(BF16)


def feed(
    place,
    block,
    normed,
    grad,
    bias,
    own_first,
    rest_first,
    own_second,
    rest_second,
    part,
    sums,
    seqs,
    shares,
):
    rows, width = normed.shape
    inside = rest_first[0].shape[0] // block
    units = rest_first[0].shape[1]
    count = own_first.shape[0] // block
    tile = min(512, units)
    skip = part * (units // tile)
    whole = pl.BlockSpec((rows, width), lambda t, k: (0, 0), pipeline_mode=pl.Buffered(1))

    def first_spec(p):
        return pl.BlockSpec((block, tile), lambda t, k: (p ^ k[0], t + skip))

    def second_spec(p):
        return pl.BlockSpec((tile, block), lambda t, k: (t + skip, p ^ k[0]))

    def first_rest(p):
        return pl.BlockSpec((block, tile), lambda t, k: (p ^ (k[0] % inside), t))

    def second_rest(p):
        return pl.BlockSpec((tile, block), lambda t, k: (t, p ^ (k[0] % inside)))

    first = [first_spec(p) for p in range(count)]
    first += [first_rest(p) for p in range(inside)] * len(rest_first)
    second = [second_spec(p) for p in range(count)]
    second += [second_rest(p) for p in range(inside)] * len(rest_second)
    unit_rows = pl.BlockSpec((rows, tile), lambda t, k: (0, t))
    return pl.pallas_call(
        functools.partial(feed_kernel, len(first), len(second), len(sums), seqs, shares),
        out_shape=[
            jax.ShapeDtypeStruct((rows, units), BF16),
            jax.ShapeDtypeStruct((rows, units), BF16),
            jax.ShapeDtypeStruct((1, units), F32),
            jax.ShapeDtypeStruct((rows, width), BF16),
            jax.ShapeDtypeStruct((rows, width), BF16),
        ],
        grid_spec=pltpu.PrefetchScalarGridSpec(
            num_scalar_prefetch=1,
            grid=(units // tile,),
            in_specs=[whole, whole, pl.BlockSpec((1, tile), lambda t, k: (0, t + skip))]
            + first
            + second
            + [whole] * len(sums),
            out_specs=[
                unit_rows,
                unit_rows,
                pl.BlockSpec((1, tile), lambda t, k: (0, t)),
                whole,
                whole,
            ],
            scratch_shapes=[pltpu.VMEM((rows, width), F32)] * 2,
        ),
        compiler_params=pltpu.CompilerParams(vmem_limit_bytes=VMEM_BYTES),
        cost_estimate=lasting(31),
        name="feed",
    )(
        place,
        normed,
        grad,
        bias,
        *([own_first] * count),
        *[piece for piece in rest_first for _ in range(inside)],
        *([own_second] * count),
        *[piece for piece in rest_second for _ in range(inside)],
        *sums,
    )


def outer_kernel(steps, adds, *refs):
    count = len(steps)
    lefts, rights = refs[: 2 * count], refs[2 * count : 3 * count]
    outs = refs[3 * count + adds : -1]
    turned = refs[-1]
    quarter = lefts[0].shape[1]
    step = pl.program_id(0)
    start = 0
    for i in range(count):

        @pl.when(step == start)
        def _():
            turned[:quarter, :] = lefts[2 * i][...].T
            turned[quarter:, :] = lefts[2 * i + 1][...].T

        @pl.when((step >= start) & (step < start + steps[i]))
        def _():
            value = nn(turned[...], rights[i][...])
            for high in range(2):
                part = value[high * quarter : (high + 1) * quarter]
                if adds:
                    part = part + refs[3 * count][high].astype(F32)
                    outs[high * count + i][...] = part.astype(BF16)
                else:
                    outs[0][high] = part.astype(BF16)

        start += steps[i]


def outer(order, pairs, low, received):
    rows, width = pairs[0][0].shape
    quarter = width // 4
    tile = min([512] + [right.shape[1] for _, right in pairs])
    steps = [right.shape[1] // tile for _, right in pairs]
    total = sum(steps) * tile
    adds = received is not None

    def left_spec(high):
        return pl.BlockSpec((rows, quarter), lambda t: (0, 2 * high + low))

    def column_spec(height, i):
        start = sum(steps[:i])
        return pl.BlockSpec((height, tile), lambda t: (0, jnp.clip(t - start, 0, steps[i] - 1)))

    both = pl.BlockSpec((2, quarter, tile), lambda t: (0, 0, t))
    if adds:
        out_shape = [
            jax.ShapeDtypeStruct((quarter, right.shape[1]), BF16) for _, right in pairs
        ] * 2
        out_specs = [column_spec(quarter, i) for i in range(len(pairs))] * 2
    else:
        out_shape = [jax.ShapeDtypeStruct((2, quarter, total), BF16)]
        out_specs = [both]
    results = pl.pallas_call(
        functools.partial(outer_kernel, steps, int(adds)),
        out_shape=out_shape,
        grid=(sum(steps),),
        in_specs=[left_spec(high) for _ in pairs for high in range(2)]
        + [column_spec(rows, i) for i in range(len(pairs))]
        + [both] * adds,
        out_specs=out_specs,
        scratch_shapes=[pltpu.VMEM((2 * quarter, rows), BF16)],
        compiler_params=pltpu.CompilerParams(vmem_limit_bytes=VMEM_BYTES),
        cost_estimate=lasting(11),
        name="outer",
    )(
        *[left for left, _ in pairs for _ in range(2)],
        *[order(right) if i == 0 else right for i, (_, right) in enumerate(pairs)],
        *([received] if adds else []),
    )
    order.mark(results[0])
    return results


def add_turned_kernel(left, right, out):
    out[...] = add_low(left[...], right[...])


def add_turned(left, right, mask, block):
    rows, width = left.shape
    tile = width
    spec = pl.BlockSpec((block, tile), lambda p, t: (p, t))
    return pl.pallas_call(
        add_turned_kernel,
        out_shape=jax.ShapeDtypeStruct((rows, width), BF16),
        grid=(rows // block, width // tile),
        in_specs=[spec, pl.BlockSpec((block, tile), lambda p, t: (p ^ mask, t))],
        out_specs=spec,
        cost_estimate=lasting(2.5),
        name="add_turned",
    )(left, right)


def finish_kernel(half, turned, groups, k_ref, *refs):
    out = refs[-1]
    pieces = refs[:-1]
    for i, piece in enumerate(pieces):
        width = piece.shape[1] // groups

        @pl.when(pl.program_id(0) // half == i % 2)
        def _():
            value = piece[...].astype(F32)
            start = i // 2 * piece.shape[1]
            if groups > 1:
                for g in range(groups):
                    out[g] = value[:, g * width : (g + 1) * width]
            elif turned:
                out[start : start + width, :] = value.T
            else:
                out[:, start : start + width] = value


def finish(place, parts, block, turned=False, groups=1):
    rows, some = parts[0][0].shape
    width = some * len(parts)
    half = rows // block
    if groups > 1:
        shape = (groups, 2 * rows, width // groups)
        out_spec = pl.BlockSpec((groups, block, width // groups), lambda p, k: (0, p ^ k[0], 0))
    elif turned:
        shape = (width, 2 * rows)
        out_spec = pl.BlockSpec((width, block), lambda p, k: (0, p ^ k[0]))
    else:
        shape = (2 * rows, width)
        out_spec = pl.BlockSpec((block, width), lambda p, k: (p ^ k[0], 0))

    def piece_spec(side):
        return pl.BlockSpec((block, some), lambda p, k: (jnp.clip(p - side * half, 0, half - 1), 0))

    return pl.pallas_call(
        functools.partial(finish_kernel, half, turned, groups),
        out_shape=jax.ShapeDtypeStruct(shape, F32),
        grid_spec=pltpu.PrefetchScalarGridSpec(
            num_scalar_prefetch=1,
            grid=(2 * half,),
            in_specs=[piece_spec(side) for _ in parts for side in (0, 1)],
            out_specs=out_spec,
        ),
        compiler_params=pltpu.CompilerParams(vmem_limit_bytes=VMEM_BYTES),
        cost_estimate=lasting(6),
        name="finish",
    )(place, *[piece for part in parts for piece in part])


def rotation_tables(positions):
    half = ROT // 2
    exponents = lax.iota(jnp.int32, half).astype(F32) * (2.0 / ROT)
    angles = positions[:, None] * jnp.power(10000.0, -exponents)[None, :]
    cosine, sine = jnp.cos(angles), jnp.sin(angles)
    ones = jnp.ones((positions.shape[0], HD - ROT), F32)
    none = jnp.zeros_like(ones)
    nought = jnp.zeros_like(sine)
    copies = LANES // HD
    return (
        jnp.concatenate([cosine, cosine, ones] * copies, 1),
        jnp.concatenate([-sine, nought, none] * copies, 1),
        jnp.concatenate([nought, sine, none] * copies, 1),
    )


def per_device(
    tokens, ln_gain, ln_bias, w_qkv, b_qkv, w_out, b_out, w_fc1, b_fc1, w_fc2, b_fc2, cotangent
):
    seqs, length, width = tokens.shape
    size = lax.axis_size("context")
    context = lax.axis_index("context")
    shard = lax.axis_index("fsdp")
    tensor_size = lax.axis_size("tensor")
    tensor = lax.axis_index("tensor")
    across = size // 2
    place = (context & 1) * across + context // 2
    me = shard * size + place
    block = width // (2 * size)
    rows = seqs * length
    heads_width = w_out.shape[0]
    heads_local = heads_width // HD
    head_groups = min(heads_local, size)
    seq_groups = size // head_groups
    span = heads_width // head_groups
    direct = seq_groups == 1 and span % LANES == 0 and size == 4
    me_s, place_s, context_s = (jnp.reshape(v, (1,)).astype(jnp.int32) for v in (me, place, context))

    small = (ln_gain, ln_bias, b_out, b_fc2, b_fc1, b_qkv.reshape(-1))
    packed = jnp.concatenate(small)
    other = to_fsdp(packed)
    halves = 2
    units = w_fc1.shape[1] // halves

    def qkv_at(p):
        return lax.dynamic_slice_in_dim(w_qkv, (place ^ p) * block, block, 1)

    def out_at(p):
        return lax.dynamic_slice_in_dim(w_out, (place ^ p) * block, block, 1)

    flat = tokens.reshape(rows, width)
    grad_flat = cotangent.reshape(rows, width)
    both = jnp.where(shard == 0, jnp.stack([packed, other]), jnp.stack([other, packed]))
    both = both.astype(F32)
    vectors = []
    at = 0
    for value in small:
        vectors.append(both[:, at : at + value.size])
        at += value.size
    gain, bias, out_bias, fc2_bias, fc1_bias = (v.reshape(1, -1) for v in vectors[:5])
    qkv_bias = jnp.swapaxes(vectors[5].reshape(2, 3, -1), 0, 1).reshape(3, 1, heads_width)
    normed, grad, bias_sum = prepare(me_s, 2 * size, flat, grad_flat, gain, bias)
    positions = (context * length + lax.iota(jnp.int32, length)).astype(F32)
    tables = rotation_tables(positions)
    bias_sum, *tables = lax.optimization_barrier((bias_sum, *tables))

    order = Order()
    half = across * block
    core = context & 1

    def fc_from(i, *done):
        first = lax.dynamic_slice(w_fc1, (core * half, i * units), (half, units))
        second = lax.dynamic_slice(w_fc2, (i * units, core * half), (units, half))
        return to_fsdp(after(first, *done)), to_fsdp(after(second, *done))

    first_mine = [
        lax.dynamic_slice(w_fc1, (core * half, i * units), (half, units)) for i in range(halves)
    ]
    second_mine = [
        lax.dynamic_slice(w_fc2, (i * units, core * half), (units, half)) for i in range(halves)
    ]
    rest_qkv = [to_fsdp(qkv_at(0))]
    ready = rest_qkv[0]
    rest_out = [to_fsdp(after(out_at(0), ready))]
    first_near = [to_fsdp(after(first_mine[0], ready))]
    order.mark(bias_sum)
    for mask in masks_of(across):
        rest_qkv = rest_qkv + [to_context(piece, 2 * mask) for piece in rest_qkv]
    mine = first_mine[1:] + second_mine
    waited = order.wait(*rest_qkv, *rest_out, *mine)
    rest_qkv, rest_out = list(waited[:across]), list(waited[across : -len(mine)])
    first_mine[1:], second_mine = waited[-len(mine) : -halves], waited[-halves:]
    for mask in masks_of(across):
        rest_out = rest_out + [to_context(piece, 2 * mask) for piece in rest_out]
    rest_qkv = rest_qkv + [to_context(piece, 1) for piece in rest_qkv]
    waited = order.wait(first_near[0], *rest_out)
    first_near[0], rest_out = waited[0], list(waited[1:])
    rest_out = rest_out + [to_context(piece, 1) for piece in rest_out]
    second_near = [to_fsdp(after(second_mine[0], first_near[0]))]

    def first_from(i, *done):
        return to_fsdp(after(first_mine[i], *done))

    def second_from(i, *done):
        return to_fsdp(after(second_mine[i], *done))

    near = jnp.concatenate([out_at(p) for p in range(across)] + rest_out[:across], 1)
    near = lax.all_gather(near, "tensor", axis=0, tiled=True)

    pieces = project(
        place_s,
        context_s,
        order(normed),
        grad,
        w_qkv,
        rest_qkv,
        w_out,
        rest_out,
        qkv_bias,
        tables,
        seqs,
        size if direct else 1,
    )
    def send_across(own, beside, across_pair):
        return own, beside, to_context(across_pair, 2)

    def pass_on(own, beside, far_pair):
        (far_pair,) = order.wait(far_pair)
        return [own, to_context(order(beside), 1), far_pair[:1], to_context(far_pair[1:], 1)]

    if direct:
        here = [send_across(*pieces[0])]
    else:
        field = jnp.concatenate([row[0] for row in pieces], 0)

        def part_for(mask):
            target = context ^ mask
            starts = [0] * 4
            sizes = list(field.shape)
            starts[0] = (target // head_groups) * (seqs // seq_groups)
            sizes[0] = seqs // seq_groups
            starts[3] = (target % head_groups) * span
            sizes[3] = span
            return lax.dynamic_slice(field, starts, sizes)

        here = [[part_for(0)] + [to_context(part_for(m), m) for m in range(1, size)]]

    order.mark(pieces[0][0])

    sums = ()
    fed_parts = []
    back = []

    def feed_part(i, sums):
        first, second = first_near[i], second_near[i]
        hidden, pre_grad, pre_sum, *sums = feed(
            place_s,
            block,
            order(normed),
            grad,
            fc1_bias,
            w_fc1,
            [first, to_context(first, 1)],
            w_fc2,
            [second, to_context(second, 1)],
            i,
            tuple(sums),
            *((seqs, tensor_size) if i == halves - 1 else (1, 1)),
        )
        fed_parts.append((hidden, pre_grad, order.mark(pre_sum)))
        return sums

    rows_here = list(here)
    for i in range(max(halves, len(pieces) if direct else 1)):
        if i < halves:
            (second_near[i],) = order.wait(second_near[i])
            if i + 1 < halves:
                first_near.append(first_from(i + 1, second_near[i]))
            sums = feed_part(i, sums)
            if i + 1 < halves:
                (first_near[i + 1],) = order.wait(first_near[i + 1])
                second_near.append(second_from(i + 1, first_near[i + 1]))
        if i == halves - 1:
            fed, fed_back = sums
            fed_share = lax.psum_scatter(fed, "tensor", scatter_dimension=0, tiled=True)
            fc_sums = [
                Reduction(order, ((normed, part[1]), (grad, part[0])), block)
                for part in fed_parts
            ]
            if direct and 0 < i < len(rows_here):
                rows_here[i] = list(order.wait(*rows_here[i]))
            fc_sums[0].send()
        if i < len(here):
            if direct and i == 0:
                rows_here = [pass_on(*here[0])]
                for own, beside, across_pair in pieces[1:]:
                    across_pair = after(order(across_pair), here[-1][2])
                    here.append(send_across(own, beside, across_pair))
            row = rows_here[i]
            result = attend(context_s, [order(row[0])] + row[1:], direct)
            order.mark(result[0])
            if direct:
                back.append(send_across(*result))
                if i + 1 < len(here):
                    rows_here.append(pass_on(*here[i + 1]))
            else:
                back.append(
                    [result[0]] + [to_context(result[m], m) for m in range(1, size)]
                )
    if not direct:
        stacked = jnp.stack(back[0])
        sources = lax.iota(jnp.int32, size) ^ context
        ordered = jnp.take(stacked, sources, axis=0)
        ordered = ordered.reshape(seq_groups, head_groups, seqs // seq_groups, 4, length, span)
        ordered = jnp.transpose(ordered, (0, 2, 3, 4, 1, 5))
        ordered = ordered.reshape(seqs, 4, length, heads_width)
        back = [[ordered[s : s + 1]] for s in range(seqs)]

    share = rows // tensor_size

    def turn_back(s, unturned):
        row = [order(back[s][0])] + back[s][1:]
        results = unturn(context_s, row, tables, s, rows, tuple(unturned))
        order.mark(results[0])
        return results

    def add_heads(s, raw_grad, norm_terms):
        return order.mark(
            norm_back(
                place_s,
                order(raw_grad),
                fed_back,
                w_qkv,
                rest_qkv,
                s,
                seqs,
                tensor_size,
                tuple(norm_terms),
            )
        )

    part_rows = length // tensor_size

    def heads_of(s, merged):
        def rows_for(mask):
            start = s * length + (tensor ^ mask) * part_rows
            return lax.dynamic_slice_in_dim(merged, start, part_rows, 0)

        return [rows_for(0)] + [to_tensor(rows_for(m), m) for m in range(1, tensor_size)]

    def arrived(*values):
        return order.wait(*values)

    first_sum, second_sum = fc_sums
    if direct:
        back[0] = pass_on(*back[0])
    unturned = []
    norm_terms = ()
    heads_from = []
    qkv_bias_sum = 0.0
    for s in range(seqs):
        *unturned, part_sum = turn_back(s, unturned)
        qkv_bias_sum = qkv_bias_sum + part_sum
        heads_from.append(heads_of(s, unturned[0]))
        norm_terms = [add_heads(s, unturned[1], norm_terms)]
        if s == 0:
            first_sum.keep()
            first_sum.over_fsdp(0)
        if direct and s + 1 < seqs:
            back[s + 1] = pass_on(*back[s + 1])
    merged, raw_grad = unturned
    last_sum = Reduction(order, ((grad, merged), (normed, raw_grad)), block)
    arrivals = arrived(*[piece for pieces_here in heads_from for piece in pieces_here[1:]])
    norm_share = order(norm_terms[0]).reshape(rows, width)
    norm_share = lax.psum_scatter(norm_share, "tensor", scatter_dimension=0, tiled=True)
    second_sum.send()
    (first_sum.far[0],) = arrived(first_sum.far[0])
    first_sum.over_fsdp(1, first_sum.far[0])
    first_sum.over_chips(0)

    def in_order(blocks):
        return jnp.concatenate(own_blocks(blocks, 1, me, block), 1).astype(F32)

    def shared_rows(value):
        return lax.dynamic_slice_in_dim(value, tensor * part_rows, part_rows, 1).reshape(share, width)

    def from_shares(value):
        value = value.reshape(tensor_size, seqs, part_rows, width)
        return jnp.swapaxes(value, 0, 1).reshape(tokens.shape)

    inputs = shared_rows(tokens).astype(F32)
    all_heads = jnp.zeros((share, tensor_size * heads_width), BF16)
    arrivals = list(arrivals)
    for s in range(seqs):
        for m in range(tensor_size):
            piece = arrivals.pop(0) if m else heads_from[s][0]
            all_heads = lax.dynamic_update_slice(
                all_heads, order(piece), (s * part_rows, (tensor ^ m) * heads_width)
            )
    far = to_context(near, 1)
    near_part, far_part = nn(all_heads, near), nn(all_heads, far)
    attended = [near_part[:, :half], far_part[:, :half], near_part[:, half:], far_part[:, half:]]
    branch_sum = in_order(jnp.concatenate(attended, 1) + fed_share.astype(F32))
    block_out = (inputs + branch_sum + out_bias + fc2_bias).astype(BF16)
    order.mark(block_out)
    block_out = from_shares(lax.all_gather(block_out, "tensor", axis=0, tiled=True))
    second_sum.keep()
    last_sum.send()
    first_sum.far[1], first_sum.far[0] = arrived(first_sum.far[1], first_sum.far[0])
    second_sum.over_fsdp(0, first_sum.far[1])
    first_sum.over_chips(1)
    first_sum.over_cores(0)

    normed_grad = in_order(order(norm_share))
    centered = inputs - jnp.mean(inputs, -1, keepdims=True)
    root = lax.rsqrt(jnp.mean(centered * centered, -1, keepdims=True) + EPSILON)
    unit = centered * root
    scaled = normed_grad * gain
    inner = jnp.mean(scaled * unit, -1, keepdims=True)
    input_part = root * (scaled - jnp.mean(scaled, -1, keepdims=True) - unit * inner)
    grad_share = shared_rows(cotangent).astype(F32)
    tokens_grad = (grad_share + input_part).astype(BF16)
    norm_sums = jnp.stack([jnp.sum(normed_grad * unit, 0), jnp.sum(normed_grad, 0)])
    order.mark(norm_sums)
    order.mark(tokens_grad)
    small_sums = [norm_sums.reshape(1, -1), bias_sum] + [part[2] for part in fed_parts]
    small_sums = jnp.concatenate(small_sums + [qkv_bias_sum], 1)
    small_other = to_context(small_sums, 1)

    second_sum.far[0], first_sum.far[1], small_other = arrived(
        second_sum.far[0], first_sum.far[1], small_other
    )
    small_sums = small_sums + small_other
    small_other = to_fsdp(small_sums)
    second_sum.over_fsdp(1, second_sum.far[0])
    second_sum.over_chips(0)
    first_sum.over_cores(1)
    last_sum.keep()
    second_sum.far[1], second_sum.far[0], small_other = arrived(
        second_sum.far[1], second_sum.far[0], small_other
    )
    small_sums = small_sums + small_other
    for mask in masks_of(across):
        small_sums = small_sums + to_context(small_sums, 2 * mask)
    last_sum.over_fsdp(1, second_sum.far[1])
    second_sum.over_chips(1)
    second_sum.over_cores(0)
    norm_sums = order.mark(small_sums)[0, : 2 * width].reshape(2, width)
    high = norm_sums.astype(BF16)
    low = (norm_sums - high.astype(F32)).astype(BF16)
    extra = jnp.concatenate([high, low, jnp.zeros((12, width), BF16)], 0)
    gathered = jnp.concatenate([order(tokens_grad), extra], 0)
    gathered = lax.all_gather(gathered, "tensor", axis=0, tiled=False)
    tokens_grad = from_shares(gathered[:, :share])
    norm_sums = jnp.sum(gathered[:, share : share + 4].astype(F32), 0)
    norm_sums = norm_sums[:2] + norm_sums[2:]
    fc1_grad = order.mark(
        finish(place_s, [first_sum.pieces[0], second_sum.pieces[0]], block)
    )
    last_sum.far[1], second_sum.far[1] = arrived(last_sum.far[1], second_sum.far[1])
    last_sum.over_fsdp(0, last_sum.far[1])
    last_sum.over_chips(1)
    second_sum.over_cores(1)
    fc2_grad = order.mark(
        finish(place_s, [first_sum.pieces[1], second_sum.pieces[1]], block, turned=True)
    )
    (last_sum.far[0],) = arrived(last_sum.far[0])
    last_sum.over_chips(0)
    last_sum.over_cores(1)
    qkv_grad = order.mark(finish(place_s, [last_sum.pieces[1]], block, groups=3))
    last_sum.over_cores(0)
    out_grad = order.mark(finish(place_s, [last_sum.pieces[0]], block, turned=True))
    units_here = b_fc1.shape[0] * 2
    small_sums = small_sums[0]
    other_sums = small_sums[2 * width :]

    def shard_of(value):
        part = value.shape[-1] // 2
        return lax.dynamic_slice_in_dim(value, shard * part, part, value.ndim - 1)

    out_bias_grad = shard_of(other_sums[:width])
    fc1_bias_grad = shard_of(other_sums[width : width + units_here])
    qkv_bias_grad = shard_of(other_sums[width + units_here :].reshape(3, heads_width))
    return (
        block_out,
        tokens_grad,
        shard_of(norm_sums[0]),
        shard_of(norm_sums[1]),
        qkv_grad,
        qkv_bias_grad,
        out_grad,
        out_bias_grad,
        fc1_grad,
        fc1_bias_grad,
        fc2_grad,
        out_bias_grad,
    )


def solution(mesh):
    return jax.shard_map(
        per_device,
        mesh=mesh,
        in_specs=(
            P("fsdp", "context", None),
            P("fsdp"),
            P("fsdp"),
            P(None, "fsdp", "tensor"),
            P(None, ("tensor", "fsdp")),
            P("tensor", "fsdp"),
            P("fsdp"),
            P("fsdp", "tensor"),
            P(("tensor", "fsdp")),
            P("tensor", "fsdp"),
            P("fsdp"),
            P("fsdp", "context", None),
        ),
        out_specs=(
            P("fsdp", "context", None),
            P("fsdp", "context", None),
            P("fsdp"),
            P("fsdp"),
            P(None, "fsdp", "tensor"),
            P(None, ("tensor", "fsdp")),
            P("tensor", "fsdp"),
            P("fsdp"),
            P("fsdp", "tensor"),
            P(("tensor", "fsdp")),
            P("tensor", "fsdp"),
            P("fsdp"),
        ),
        check_vma=False,
    )
```

```python
import functools

import jax
import jax.numpy as jnp
from jax import lax
import jax.experimental.pallas as pl
import jax.experimental.pallas.tpu as pltpu
from jax.sharding import PartitionSpec as P

HD = 64
ROT = 32
EPSILON = 1e-05
LANES = 128
F32 = jnp.float32
BF16 = jnp.bfloat16
ROOT = 0.7978845608028654
CUBE = 0.044715
VMEM_BYTES = 60 << 20


def lasting(micros):
    return pl.CostEstimate(flops=0, bytes_accessed=int(micros * 3.4e6), transcendentals=0)


def nn(a, b):
    return lax.dot_general(a, b, (((1,), (0,)), ((), ())), preferred_element_type=F32)


def nt(a, b):
    return lax.dot_general(a, b, (((1,), (1,)), ((), ())), preferred_element_type=F32)


def tn(a, b):
    return lax.dot_general(a, b, (((0,), (0,)), ((), ())), preferred_element_type=F32)


def add_low(*terms):
    total = terms[0].astype(F32)
    for term in terms[1:]:
        total = total + term.astype(F32)
    return total.astype(BF16)


def to_fsdp(value):
    return lax.ppermute(value, "fsdp", [(0, 1), (1, 0)])


def to_context(value, mask):
    size = lax.axis_size("context")
    return lax.ppermute(value, "context", [(i, i ^ mask) for i in range(size)])


def to_tensor(value, mask):
    size = lax.axis_size("tensor")
    return lax.ppermute(value, "tensor", [(i, i ^ mask) for i in range(size)])


def after(value, *others):
    return lax.optimization_barrier((value,) + others)[0]


def masks_of(size):
    mask = 1
    while mask < size:
        yield mask
        mask *= 2


def own_blocks(own, axis, place, block):
    count = own.shape[axis] // block
    return [
        lax.dynamic_slice_in_dim(own, (p ^ place) * block, block, axis) for p in range(count)
    ]


class Order:
    def __init__(self):
        self.last = None

    def __call__(self, value):
        return value if self.last is None else after(value, self.last)

    def mark(self, value):
        self.last = value
        return value

    def wait(self, *values):
        if self.last is not None:
            values = lax.optimization_barrier(values + (self.last,))[:-1]
        else:
            values = lax.optimization_barrier(values)
        self.last = values[0]
        return values


class Reduction:
    def __init__(self, order, pairs, block):
        self.order, self.pairs, self.block = order, pairs, block

    def compute(self):
        (self.sent,) = outer(self.order, self.pairs, 1, None)

    def send(self):
        self.compute()
        self.sent = to_context(self.sent, 1)

    def keep(self):
        results = outer(self.order, self.pairs, 0, self.sent)
        self.near, self.far = results[: len(self.pairs)], results[len(self.pairs) :]
        self.near, self.far = list(self.near), list(self.far)
        self.pieces = [None] * len(self.pairs)

    def over_fsdp(self, i, *earlier):
        self.far[i] = to_fsdp(after(self.far[i], *earlier) if earlier else self.far[i])
        return self.far[i]

    def over_chips(self, i):
        self.near[i] = self.order.mark(add_low(self.order(self.near[i]), self.far[i]))
        self.masks = list(masks_of(lax.axis_size("context") // 2))
        if self.masks:
            self.far[i] = to_context(self.near[i], 2 * self.masks[0])
        return self.far[i]

    def over_cores(self, i):
        total = self.near[i]
        for n, mask in enumerate(self.masks):
            other = self.far[i] if n == 0 else to_context(total, 2 * mask)
            total = self.order.mark(add_turned(self.order(total), other, mask, self.block))
        self.pieces[i] = (total, to_context(total, 1))


def prepare_kernel(count, me_ref, tokens, grad, gain, bias, normed_out, grad_out, sum_out, kept):
    values = tokens[...].astype(F32)
    centered = values - jnp.mean(values, -1, keepdims=True)
    variance = jnp.mean(centered * centered, -1, keepdims=True)
    kept[...] = (centered * lax.rsqrt(variance + EPSILON) * gain[...] + bias[...]).astype(BF16)
    me = me_ref[0]
    block = tokens.shape[1] // count
    for p in range(count):
        source = pl.ds(pl.multiple_of((p ^ me) * block, block), block)
        normed_out[:, p * block : (p + 1) * block] = kept[:, source]
        grad_out[:, p * block : (p + 1) * block] = grad[:, source]
    part = jnp.sum(grad[...].astype(F32), 0, keepdims=True)

    @pl.when(pl.program_id(0) == 0)
    def _():
        sum_out[...] = part

    @pl.when(pl.program_id(0) > 0)
    def _():
        sum_out[...] += part


def prepare(me, count, tokens, grad, gain, bias):
    rows, width = tokens.shape
    tile = min(128, rows)
    row_spec = pl.BlockSpec((tile, width), lambda r, me: (r, 0))
    one_spec = pl.BlockSpec((1, width), lambda r, me: (0, 0))
    return pl.pallas_call(
        functools.partial(prepare_kernel, count),
        out_shape=[
            jax.ShapeDtypeStruct((rows, width), BF16),
            jax.ShapeDtypeStruct((rows, width), BF16),
            jax.ShapeDtypeStruct((1, width), F32),
        ],
        grid_spec=pltpu.PrefetchScalarGridSpec(
            num_scalar_prefetch=1,
            grid=(rows // tile,),
            in_specs=[row_spec, row_spec, one_spec, one_spec],
            out_specs=[row_spec, row_spec, one_spec],
            scratch_shapes=[pltpu.VMEM((tile, width), BF16)],
        ),
        compiler_params=pltpu.CompilerParams(vmem_limit_bytes=VMEM_BYTES),
        cost_estimate=lasting(10),
        name="prepare",
    )(me, tokens, grad, gain, bias)


def turn(part, cosine, below, above):
    return (
        part * cosine
        + pltpu.roll(part, LANES - ROT // 2, 1) * below
        + pltpu.roll(part, ROT // 2, 1) * above
    )


def project_kernel(seqs, qkv_count, out_count, parts, k_ref, c_ref, *refs):
    normed, grad, bias, cosine, below, above = refs[:6]
    ends = (6 + qkv_count, 6 + qkv_count + out_count)
    outs, kept = refs[ends[1] : -1], refs[-1]
    which = pl.program_id(0)
    rows, width = kept.shape
    length = rows // seqs

    @pl.when(which < 3)
    def _():
        weight = jnp.concatenate([w[0] for w in refs[6 : ends[0]]], 0)
        raw = nn(normed[...], weight) + bias[0]

        @pl.when(which < 2)
        def _():
            for s in range(seqs):
                for lane in range(0, width, LANES):
                    part = raw[s * length : (s + 1) * length, lane : lane + LANES]
                    kept[s * length : (s + 1) * length, lane : lane + LANES] = turn(
                        part, cosine[...], below[...], above[...]
                    ).astype(BF16)

        @pl.when(which == 2)
        def _():
            kept[...] = raw.astype(BF16)

    @pl.when(which == 3)
    def _():
        weight = jnp.concatenate([w[...] for w in refs[ends[0] : ends[1]]], 1)
        kept[...] = nt(grad[...], weight).astype(BF16)

    span = width // parts
    for m in range(parts):
        at = pl.ds(pl.multiple_of((m ^ c_ref[0]) * span, span), span) if parts > 1 else slice(None)
        for s in range(seqs):
            part = kept[s * length : (s + 1) * length, at]
            if parts == 1:
                outs[s][0, 0] = part
            else:
                outs[3 * s + min(m, 2)][max(m - 2, 0), 0] = part


def project(place, context, normed, grad, qkv, qkv_rest, out, out_rest, bias, tables, seqs, parts):
    rows, depth = normed.shape
    width = qkv.shape[2]
    block = qkv_rest[0].shape[1]
    count = qkv.shape[1] // block
    length = rows // seqs
    span = width // parts
    table = pl.BlockSpec((length, LANES), lambda c, k, x: (0, 0))
    whole = pl.BlockSpec((rows, depth), lambda c, k, x: (0, 0), pipeline_mode=pl.Buffered(1))

    def qkv_spec(p):
        return pl.BlockSpec((1, block, width), lambda c, k, x: (jnp.minimum(c, 2), p ^ k[0], 0))

    def out_spec(p):
        return pl.BlockSpec((width, block), lambda c, k, x: (0, p ^ k[0]))

    qkv_specs = [qkv_spec(p) for p in range(count)] + [
        pl.BlockSpec((1, block, width), lambda c, k, x: (jnp.minimum(c, 2), 0, 0))
    ] * len(qkv_rest)
    out_specs = [out_spec(p) for p in range(count)] + [
        pl.BlockSpec((width, block), lambda c, k, x: (0, 0))
    ] * len(out_rest)
    counts = [1] if parts == 1 else [1, 1, 2]
    results = pl.pallas_call(
        functools.partial(project_kernel, seqs, len(qkv_specs), len(out_specs), parts),
        out_shape=[jax.ShapeDtypeStruct((n, 4, length, span), BF16) for n in counts] * seqs,
        grid_spec=pltpu.PrefetchScalarGridSpec(
            num_scalar_prefetch=2,
            grid=(4,),
            in_specs=[
                whole,
                whole,
                pl.BlockSpec((1, 1, width), lambda c, k, x: (jnp.minimum(c, 2), 0, 0)),
                table,
                table,
                table,
            ]
            + qkv_specs
            + out_specs,
            out_specs=[
                pl.BlockSpec((n, 1, length, span), lambda c, k, x: (0, c, 0, 0)) for n in counts
            ]
            * seqs,
            scratch_shapes=[pltpu.VMEM((rows, width), BF16)],
        ),
        compiler_params=pltpu.CompilerParams(vmem_limit_bytes=VMEM_BYTES),
        cost_estimate=lasting(19),
        name="project",
    )(
        place,
        context,
        normed,
        grad,
        bias,
        *tables,
        *([qkv] * count),
        *qkv_rest,
        *([out] * count),
        *out_rest,
    )
    return [results[s * len(counts) : (s + 1) * len(counts)] for s in range(seqs)]


def attend_kernel(parts, bq, bk, me_ref, *refs):
    pieces = refs[:parts]
    outs = refs[parts:-11]
    q_all, k_all, v_all, g_all, v_turned, k_turned, o_all, dq_all, dk_all, dv_all, held = refs[-11:]
    rows, width = pieces[0].shape[2:]
    length = rows * parts
    me = me_ref[0]
    scale = HD**-0.5
    for m in range(parts):
        at = pl.ds(pl.multiple_of((me ^ m) * rows, rows), rows)
        q_all[at, :] = (pieces[m][0, 0].astype(F32) * scale).astype(BF16)
        k_all[at, :] = pieces[m][0, 1]
        v_all[at, :] = pieces[m][0, 2]
        g_all[at, :] = pieces[m][0, 3]
    v_turned[...] = v_all[...].T
    k_turned[...] = k_all[...].T
    dk_all[...] = jnp.zeros_like(dk_all)
    dv_all[...] = jnp.zeros_like(dv_all)
    heads = width // HD
    lane_head = lax.broadcasted_iota(jnp.int32, (1, width), 1) // HD

    for first in range(0, length, bq):
        at_q = slice(first, first + bq)
        query, grad = q_all[at_q, :], g_all[at_q, :]
        spans = [slice(k, min(k + bk, first + bq)) for k in range(0, first + bq, bk)]
        outputs, q_grads = [], []
        for h in range(heads):
            at_h = slice(h * HD, (h + 1) * HD)
            q_head = jnp.where(lane_head == h, query, jnp.zeros_like(query))
            g_head = jnp.where(lane_head == h, grad, jnp.zeros_like(grad))
            top = jnp.full((8, bq), -1e30, F32)
            for span in spans:
                scores = nt(k_all[span, :], q_head)
                free = min(span.stop, max(first, span.start)) - span.start
                if free:
                    part = scores[:free]
                    held[span.start : span.start + free, :] = part
                    top = jnp.maximum(top, jnp.max(part.reshape(free // 8, 8, bq), 0))
                rest = span.stop - span.start - free
                if rest:
                    key = span.start + free + lax.broadcasted_iota(jnp.int32, (rest, bq), 0)
                    place = first + lax.broadcasted_iota(jnp.int32, (rest, bq), 1)
                    part = jnp.where(key <= place, scores[free:], -1e30)
                    held[span.start + free : span.stop, :] = part
                    top = jnp.maximum(top, jnp.max(part.reshape(rest // 8, 8, bq), 0))
            top = jnp.max(top, 0, keepdims=True)
            total = jnp.zeros((8, bq), F32)
            output = jnp.zeros((HD, bq), F32)
            for span in spans:
                weights = jnp.exp(held[span, :] - top)
                held[span, :] = weights
                total = total + jnp.sum(weights.reshape(-1, 8, bq), 0)
                output = output + nn(v_turned[at_h, span], weights.astype(BF16))
            inverse = 1.0 / jnp.sum(total, 0, keepdims=True)
            output = output * inverse
            g_turned = g_head.T.astype(F32)
            inner = jnp.sum(output * g_turned[at_h], 0, keepdims=True) * inverse
            g_scaled = (g_turned * inverse).astype(BF16)
            g_rows = g_scaled.T
            q_grad = jnp.zeros((HD, bq), F32)
            for span in spans:
                weights = held[span, :]
                prob_grad = nn(v_all[span, :], g_scaled)
                score_grad = (weights * (prob_grad - inner)).astype(BF16)
                dv_all[span, :] += nn(weights.astype(BF16), g_rows)
                dk_all[span, :] += nn(score_grad, q_head)
                q_grad = q_grad + nn(k_turned[at_h, span], score_grad)
            outputs.append(output)
            q_grads.append(q_grad * scale)
        o_all[at_q, :] = jnp.concatenate(outputs, 0).T.astype(BF16)
        dq_all[at_q, :] = jnp.concatenate(q_grads, 0).T.astype(BF16)
    for m in range(parts):
        at = pl.ds(pl.multiple_of((me ^ m) * rows, rows), rows)
        out, i = (outs[m], 0) if len(outs) == parts else (outs[min(m, 2)], max(m - 2, 0))
        out[i, 0] = o_all[at, :]
        out[i, 1] = dq_all[at, :]
        out[i, 2] = dk_all[at, :].astype(BF16)
        out[i, 3] = dv_all[at, :].astype(BF16)


def attend(context, pieces, paired):
    parts = len(pieces)
    seqs, _, rows, width = pieces[0].shape
    length = rows * parts
    bq = min(512, length)
    bk = min(2048, length)
    vmem = pltpu.VMEM
    counts = [1, 1, 2] if paired else [seqs] * parts
    return pl.pallas_call(
        functools.partial(attend_kernel, parts, bq, bk),
        out_shape=[jax.ShapeDtypeStruct((n, 4, rows, width), BF16) for n in counts],
        grid_spec=pltpu.PrefetchScalarGridSpec(
            num_scalar_prefetch=1,
            grid=(seqs,),
            in_specs=[pl.BlockSpec((1, 4, rows, width), lambda s, me: (s, 0, 0, 0))] * parts,
            out_specs=[
                pl.BlockSpec((n if paired else 1, 4, rows, width), lambda s, me: (s, 0, 0, 0))
                for n in counts
            ],
            scratch_shapes=[vmem((length, width), BF16)] * 4
            + [vmem((width, length), BF16)] * 2
            + [vmem((length, width), BF16)] * 2
            + [vmem((length, width), F32)] * 2
            + [vmem((length, bq), F32)],
        ),
        compiler_params=pltpu.CompilerParams(vmem_limit_bytes=VMEM_BYTES),
        cost_estimate=lasting(28),
        name="attend",
    )(context, *pieces)


def unturn_kernel(parts, c_ref, *refs):
    pieces = refs[:parts]
    cosine, below, above = refs[parts : parts + 3]
    merged, raw, sums = refs[-3:]
    width = merged.shape[1]
    span = width // parts
    for m in range(parts):
        at = pl.ds(pl.multiple_of((m ^ c_ref[0]) * span, span), span) if parts > 1 else slice(None)
        merged[:, at] = pieces[m][0, 0]
    for c in range(3):
        for m in range(parts):
            for lane in range(0, span, LANES):
                start = (m ^ c_ref[0]) * span + c * width + lane if parts > 1 else c * width + lane
                at = pl.ds(pl.multiple_of(start, LANES), LANES)
                part = pieces[m][0, c + 1, :, lane : lane + LANES]
                if c < 2:
                    part = turn(part.astype(F32), cosine[...], -below[...], -above[...])
                    part = part.astype(BF16)
                raw[:, at] = part
                sums[:, at] = jnp.sum(part.astype(F32), 0, keepdims=True)


def unturn(context, pieces, tables, s, rows, earlier):
    parts = len(pieces)
    length, span = pieces[0].shape[2:]
    width = span * parts
    vmem = pl.BlockSpec(memory_space=pltpu.VMEM)
    return pl.pallas_call(
        functools.partial(unturn_kernel, parts),
        out_shape=[
            jax.ShapeDtypeStruct((rows, width), BF16),
            jax.ShapeDtypeStruct((rows, 3 * width), BF16),
            jax.ShapeDtypeStruct((1, 3 * width), F32),
        ],
        grid=(1,),
        in_specs=[pl.BlockSpec(memory_space=pltpu.SMEM)]
        + [vmem] * (parts + 3)
        + [pl.BlockSpec(memory_space=pl.ANY)] * len(earlier),
        out_specs=[
            pl.BlockSpec((length, width), lambda i: (s, 0)),
            pl.BlockSpec((length, 3 * width), lambda i: (s, 0)),
            vmem,
        ],
        input_output_aliases={parts + 4 + i: i for i in range(len(earlier))},
        compiler_params=pltpu.CompilerParams(vmem_limit_bytes=VMEM_BYTES),
        cost_estimate=lasting(4),
        name="unturn",
    )(context, *pieces, *tables, *earlier)


def norm_back_kernel(count, k_ref, raw, back, *refs):
    out, total = refs[-2:]
    weight = jnp.concatenate([w[0] for w in refs[:count]], 0)
    term = nt(raw[...], weight)
    step = pl.program_id(0)

    @pl.when(step == 0)
    def _():
        total[...] = back[...].astype(F32) + term

    @pl.when(step == 1)
    def _():
        total[...] += term

    @pl.when(step == 2)
    def _():
        out[...] = (total[...] + term).astype(BF16).reshape(out.shape)


def norm_back(place, raw, back, own, rest, s, seqs, shares, earlier):
    rows, depth = back.shape
    width = own.shape[2]
    block = rest[0].shape[1]
    count = own.shape[1] // block
    length = rows // seqs

    def own_spec(p):
        return pl.BlockSpec((1, block, width), lambda c, k: (c, p ^ k[0], 0))

    specs = [own_spec(p) for p in range(count)] + [
        pl.BlockSpec((1, block, width), lambda c, k: (c, 0, 0))
    ] * len(rest)
    return pl.pallas_call(
        functools.partial(norm_back_kernel, len(specs)),
        out_shape=jax.ShapeDtypeStruct((shares, seqs, length // shares, depth), BF16),
        grid_spec=pltpu.PrefetchScalarGridSpec(
            num_scalar_prefetch=1,
            grid=(3,),
            in_specs=[
                pl.BlockSpec((length, width), lambda c, k: (s, c)),
                pl.BlockSpec((length, depth), lambda c, k: (s, 0)),
            ]
            + specs
            + [pl.BlockSpec(memory_space=pl.ANY)] * len(earlier),
            out_specs=pl.BlockSpec(
                (shares, 1, length // shares, depth), lambda c, k: (0, s, 0, 0)
            ),
            scratch_shapes=[pltpu.VMEM((length, depth), F32)],
        ),
        input_output_aliases={3 + len(specs) + i: i for i in range(len(earlier))},
        compiler_params=pltpu.CompilerParams(vmem_limit_bytes=VMEM_BYTES),
        cost_estimate=lasting(8),
        name="norm_back",
    )(place, raw, back, *([own] * count), *rest, *earlier)


def gelu_pair(value):
    square = value * value
    bent = jnp.tanh(ROOT * value * (1.0 + CUBE * square))
    half = 0.5 * (1.0 + bent)
    slope = half + 0.5 * value * (1.0 - bent * bent) * (ROOT * (1.0 + 3.0 * CUBE * square))
    return value * half, slope


def feed_kernel(first_count, second_count, onto, seqs, shares, k_ref, *refs):
    normed, grad, bias = refs[:3]
    ends = (3 + first_count, 3 + first_count + second_count)
    first = jnp.concatenate([r[...] for r in refs[3 : ends[0]]], 0)
    second = jnp.concatenate([r[...] for r in refs[ends[0] : ends[1]]], 1)
    hidden_out, pre_grad_out, sum_out, fed_out, back_out, fed, back = refs[ends[1] + onto :]
    tile = pl.program_id(0)

    @pl.when(tile == 0)
    def _():
        if onto:
            fed[...] = refs[ends[1]][...].astype(F32)
            back[...] = refs[ends[1] + 1][...].astype(F32)
        else:
            fed[...] = jnp.zeros_like(fed)
            back[...] = jnp.zeros_like(back)

    hidden, slope = gelu_pair(nn(normed[...], first) + bias[...])
    hidden_low = hidden.astype(BF16)
    pre_grad = (nt(grad[...], second) * slope).astype(BF16)
    hidden_out[...] = hidden_low
    pre_grad_out[...] = pre_grad
    fed[...] += nn(hidden_low, second)
    back[...] += nt(pre_grad, first)
    sum_out[...] = jnp.sum(pre_grad.astype(F32), 0, keepdims=True)

    @pl.when(tile == pl.num_programs(0) - 1)
    def _():
        tile_rows = fed.shape[0] // (seqs * shares)
        for to in range(seqs * shares):
            source = (to % seqs * shares + to // seqs) * tile_rows
            fed_out[to * tile_rows : (to + 1) * tile_rows, :] = fed[
                source : source + tile_rows, :
            ].astype(BF16)
        back_out[...] = back[...].astype(BF16)


def feed(
    place,
    block,
    normed,
    grad,
    bias,
    own_first,
    rest_first,
    own_second,
    rest_second,
    part,
    sums,
    seqs,
    shares,
):
    rows, width = normed.shape
    inside = rest_first[0].shape[0] // block
    units = rest_first[0].shape[1]
    count = own_first.shape[0] // block
    tile = min(512, units)
    skip = part * (units // tile)
    whole = pl.BlockSpec((rows, width), lambda t, k: (0, 0), pipeline_mode=pl.Buffered(1))

    def first_spec(p):
        return pl.BlockSpec((block, tile), lambda t, k: (p ^ k[0], t + skip))

    def second_spec(p):
        return pl.BlockSpec((tile, block), lambda t, k: (t + skip, p ^ k[0]))

    def first_rest(p):
        return pl.BlockSpec((block, tile), lambda t, k: (p ^ (k[0] % inside), t))

    def second_rest(p):
        return pl.BlockSpec((tile, block), lambda t, k: (t, p ^ (k[0] % inside)))

    first = [first_spec(p) for p in range(count)]
    first += [first_rest(p) for p in range(inside)] * len(rest_first)
    second = [second_spec(p) for p in range(count)]
    second += [second_rest(p) for p in range(inside)] * len(rest_second)
    unit_rows = pl.BlockSpec((rows, tile), lambda t, k: (0, t))
    return pl.pallas_call(
        functools.partial(feed_kernel, len(first), len(second), len(sums), seqs, shares),
        out_shape=[
            jax.ShapeDtypeStruct((rows, units), BF16),
            jax.ShapeDtypeStruct((rows, units), BF16),
            jax.ShapeDtypeStruct((1, units), F32),
            jax.ShapeDtypeStruct((rows, width), BF16),
            jax.ShapeDtypeStruct((rows, width), BF16),
        ],
        grid_spec=pltpu.PrefetchScalarGridSpec(
            num_scalar_prefetch=1,
            grid=(units // tile,),
            in_specs=[whole, whole, pl.BlockSpec((1, tile), lambda t, k: (0, t + skip))]
            + first
            + second
            + [whole] * len(sums),
            out_specs=[
                unit_rows,
                unit_rows,
                pl.BlockSpec((1, tile), lambda t, k: (0, t)),
                whole,
                whole,
            ],
            scratch_shapes=[pltpu.VMEM((rows, width), F32)] * 2,
        ),
        compiler_params=pltpu.CompilerParams(vmem_limit_bytes=VMEM_BYTES),
        cost_estimate=lasting(31),
        name="feed",
    )(
        place,
        normed,
        grad,
        bias,
        *([own_first] * count),
        *[piece for piece in rest_first for _ in range(inside)],
        *([own_second] * count),
        *[piece for piece in rest_second for _ in range(inside)],
        *sums,
    )


def outer_kernel(steps, adds, *refs):
    count = len(steps)
    lefts, rights = refs[: 2 * count], refs[2 * count : 3 * count]
    outs = refs[3 * count + adds : -1]
    turned = refs[-1]
    quarter = lefts[0].shape[1]
    step = pl.program_id(0)
    start = 0
    for i in range(count):

        @pl.when(step == start)
        def _():
            turned[:quarter, :] = lefts[2 * i][...].T
            turned[quarter:, :] = lefts[2 * i + 1][...].T

        @pl.when((step >= start) & (step < start + steps[i]))
        def _():
            value = nn(turned[...], rights[i][...])
            for high in range(2):
                part = value[high * quarter : (high + 1) * quarter]
                if adds:
                    part = part + refs[3 * count][high].astype(F32)
                    outs[high * count + i][...] = part.astype(BF16)
                else:
                    outs[0][high] = part.astype(BF16)

        start += steps[i]


def outer(order, pairs, low, received):
    rows, width = pairs[0][0].shape
    quarter = width // 4
    tile = min([512] + [right.shape[1] for _, right in pairs])
    steps = [right.shape[1] // tile for _, right in pairs]
    total = sum(steps) * tile
    adds = received is not None

    def left_spec(high):
        return pl.BlockSpec((rows, quarter), lambda t: (0, 2 * high + low))

    def column_spec(height, i):
        start = sum(steps[:i])
        return pl.BlockSpec((height, tile), lambda t: (0, jnp.clip(t - start, 0, steps[i] - 1)))

    both = pl.BlockSpec((2, quarter, tile), lambda t: (0, 0, t))
    if adds:
        out_shape = [
            jax.ShapeDtypeStruct((quarter, right.shape[1]), BF16) for _, right in pairs
        ] * 2
        out_specs = [column_spec(quarter, i) for i in range(len(pairs))] * 2
    else:
        out_shape = [jax.ShapeDtypeStruct((2, quarter, total), BF16)]
        out_specs = [both]
    results = pl.pallas_call(
        functools.partial(outer_kernel, steps, int(adds)),
        out_shape=out_shape,
        grid=(sum(steps),),
        in_specs=[left_spec(high) for _ in pairs for high in range(2)]
        + [column_spec(rows, i) for i in range(len(pairs))]
        + [both] * adds,
        out_specs=out_specs,
        scratch_shapes=[pltpu.VMEM((2 * quarter, rows), BF16)],
        compiler_params=pltpu.CompilerParams(vmem_limit_bytes=VMEM_BYTES),
        cost_estimate=lasting(11),
        name="outer",
    )(
        *[left for left, _ in pairs for _ in range(2)],
        *[order(right) if i == 0 else right for i, (_, right) in enumerate(pairs)],
        *([received] if adds else []),
    )
    order.mark(results[0])
    return results


def add_turned_kernel(left, right, out):
    out[...] = add_low(left[...], right[...])


def add_turned(left, right, mask, block):
    rows, width = left.shape
    tile = width
    spec = pl.BlockSpec((block, tile), lambda p, t: (p, t))
    return pl.pallas_call(
        add_turned_kernel,
        out_shape=jax.ShapeDtypeStruct((rows, width), BF16),
        grid=(rows // block, width // tile),
        in_specs=[spec, pl.BlockSpec((block, tile), lambda p, t: (p ^ mask, t))],
        out_specs=spec,
        cost_estimate=lasting(2.5),
        name="add_turned",
    )(left, right)


def finish_kernel(half, turned, groups, k_ref, *refs):
    out = refs[-1]
    pieces = refs[:-1]
    for i, piece in enumerate(pieces):
        width = piece.shape[1] // groups

        @pl.when(pl.program_id(0) // half == i % 2)
        def _():
            value = piece[...].astype(F32)
            start = i // 2 * piece.shape[1]
            if groups > 1:
                for g in range(groups):
                    out[g] = value[:, g * width : (g + 1) * width]
            elif turned:
                out[start : start + width, :] = value.T
            else:
                out[:, start : start + width] = value


def finish(place, parts, block, turned=False, groups=1):
    rows, some = parts[0][0].shape
    width = some * len(parts)
    half = rows // block
    if groups > 1:
        shape = (groups, 2 * rows, width // groups)
        out_spec = pl.BlockSpec((groups, block, width // groups), lambda p, k: (0, p ^ k[0], 0))
    elif turned:
        shape = (width, 2 * rows)
        out_spec = pl.BlockSpec((width, block), lambda p, k: (0, p ^ k[0]))
    else:
        shape = (2 * rows, width)
        out_spec = pl.BlockSpec((block, width), lambda p, k: (p ^ k[0], 0))

    def piece_spec(side):
        return pl.BlockSpec((block, some), lambda p, k: (jnp.clip(p - side * half, 0, half - 1), 0))

    return pl.pallas_call(
        functools.partial(finish_kernel, half, turned, groups),
        out_shape=jax.ShapeDtypeStruct(shape, F32),
        grid_spec=pltpu.PrefetchScalarGridSpec(
            num_scalar_prefetch=1,
            grid=(2 * half,),
            in_specs=[piece_spec(side) for _ in parts for side in (0, 1)],
            out_specs=out_spec,
        ),
        compiler_params=pltpu.CompilerParams(vmem_limit_bytes=VMEM_BYTES),
        cost_estimate=lasting(6),
        name="finish",
    )(place, *[piece for part in parts for piece in part])


def rotation_tables(positions):
    half = ROT // 2
    exponents = lax.iota(jnp.int32, half).astype(F32) * (2.0 / ROT)
    angles = positions[:, None] * jnp.power(10000.0, -exponents)[None, :]
    cosine, sine = jnp.cos(angles), jnp.sin(angles)
    ones = jnp.ones((positions.shape[0], HD - ROT), F32)
    none = jnp.zeros_like(ones)
    nought = jnp.zeros_like(sine)
    copies = LANES // HD
    return (
        jnp.concatenate([cosine, cosine, ones] * copies, 1),
        jnp.concatenate([-sine, nought, none] * copies, 1),
        jnp.concatenate([nought, sine, none] * copies, 1),
    )


def per_device(
    tokens, ln_gain, ln_bias, w_qkv, b_qkv, w_out, b_out, w_fc1, b_fc1, w_fc2, b_fc2, cotangent
):
    seqs, length, width = tokens.shape
    size = lax.axis_size("context")
    context = lax.axis_index("context")
    shard = lax.axis_index("fsdp")
    tensor_size = lax.axis_size("tensor")
    tensor = lax.axis_index("tensor")
    across = size // 2
    place = (context & 1) * across + context // 2
    me = shard * size + place
    block = width // (2 * size)
    rows = seqs * length
    heads_width = w_out.shape[0]
    heads_local = heads_width // HD
    head_groups = min(heads_local, size)
    seq_groups = size // head_groups
    span = heads_width // head_groups
    direct = seq_groups == 1 and span % LANES == 0 and size == 4
    me_s, place_s, context_s = (jnp.reshape(v, (1,)).astype(jnp.int32) for v in (me, place, context))

    small = (ln_gain, ln_bias, b_out, b_fc2, b_fc1, b_qkv.reshape(-1))
    packed = jnp.concatenate(small)
    other = to_fsdp(packed)
    halves = 2
    units = w_fc1.shape[1] // halves

    def qkv_at(p):
        return lax.dynamic_slice_in_dim(w_qkv, (place ^ p) * block, block, 1)

    def out_at(p):
        return lax.dynamic_slice_in_dim(w_out, (place ^ p) * block, block, 1)

    flat = tokens.reshape(rows, width)
    grad_flat = cotangent.reshape(rows, width)
    both = jnp.where(shard == 0, jnp.stack([packed, other]), jnp.stack([other, packed]))
    both = both.astype(F32)
    vectors = []
    at = 0
    for value in small:
        vectors.append(both[:, at : at + value.size])
        at += value.size
    gain, bias, out_bias, fc2_bias, fc1_bias = (v.reshape(1, -1) for v in vectors[:5])
    qkv_bias = jnp.swapaxes(vectors[5].reshape(2, 3, -1), 0, 1).reshape(3, 1, heads_width)
    normed, grad, bias_sum = prepare(me_s, 2 * size, flat, grad_flat, gain, bias)
    positions = (context * length + lax.iota(jnp.int32, length)).astype(F32)
    tables = rotation_tables(positions)
    bias_sum, *tables = lax.optimization_barrier((bias_sum, *tables))

    order = Order()
    half = across * block
    core = context & 1

    def fc_from(i, *done):
        first = lax.dynamic_slice(w_fc1, (core * half, i * units), (half, units))
        second = lax.dynamic_slice(w_fc2, (i * units, core * half), (units, half))
        return to_fsdp(after(first, *done)), to_fsdp(after(second, *done))

    first_mine = [
        lax.dynamic_slice(w_fc1, (core * half, i * units), (half, units)) for i in range(halves)
    ]
    second_mine = [
        lax.dynamic_slice(w_fc2, (i * units, core * half), (units, half)) for i in range(halves)
    ]
    def spread(pieces):
        for mask in masks_of(across):
            pieces = pieces + [to_context(piece, 2 * mask) for piece in pieces]
        return pieces

    def to_both(pieces):
        return pieces + [to_context(piece, 1) for piece in pieces]

    rest_qkv = [to_fsdp(qkv_at(0))]
    ready = rest_qkv[0]
    rest_out = [to_fsdp(after(out_at(0), ready))]
    first_block = lax.dynamic_slice(w_fc1, (place * block, 0), (block, units))
    second_block = lax.dynamic_slice(w_fc2, (0, place * block), (units, block))
    first_near = [[to_fsdp(after(first_block, ready))]]
    second_near = [[to_fsdp(after(second_block, ready))]]
    order.mark(bias_sum)
    rest_qkv = spread(rest_qkv)
    mine = first_mine[1:] + second_mine[1:]
    waited = order.wait(*rest_qkv, *rest_out, *mine)
    rest_qkv, rest_out = list(waited[:across]), list(waited[across : -len(mine)])
    first_mine[1:], second_mine[1:] = waited[-len(mine) : 1 - halves], waited[1 - halves :]
    rest_out = spread(rest_out)
    rest_qkv = to_both(rest_qkv)
    waited = order.wait(first_near[0][0], second_near[0][0], *rest_out)
    rest_out = to_both(list(waited[2:]))
    first_near[0], second_near[0] = spread([waited[0]]), spread([waited[1]])
    for i in range(1, halves):
        first_near.append(to_fsdp(after(first_mine[i], waited[1])))

    near = jnp.concatenate([out_at(p) for p in range(across)] + rest_out[:across], 1)
    near = lax.all_gather(near, "tensor", axis=0, tiled=True)

    pieces = project(
        place_s,
        context_s,
        order(normed),
        grad,
        w_qkv,
        rest_qkv,
        w_out,
        rest_out,
        qkv_bias,
        tables,
        seqs,
        size if direct else 1,
    )
    def send_across(own, beside, across_pair):
        return own, beside, to_context(across_pair, 2)

    def pass_on(own, beside, far_pair):
        (far_pair,) = order.wait(far_pair)
        return [own, to_context(order(beside), 1), far_pair[:1], to_context(far_pair[1:], 1)]

    if direct:
        here = [send_across(*pieces[0])]
    else:
        field = jnp.concatenate([row[0] for row in pieces], 0)

        def part_for(mask):
            target = context ^ mask
            starts = [0] * 4
            sizes = list(field.shape)
            starts[0] = (target // head_groups) * (seqs // seq_groups)
            sizes[0] = seqs // seq_groups
            starts[3] = (target % head_groups) * span
            sizes[3] = span
            return lax.dynamic_slice(field, starts, sizes)

        here = [[part_for(0)] + [to_context(part_for(m), m) for m in range(1, size)]]

    order.mark(pieces[0][0])

    sums = ()
    fed_parts = []
    back = []

    def feed_part(i, first, second, sums):
        hidden, pre_grad, pre_sum, *sums = feed(
            place_s,
            block,
            order(normed),
            grad,
            fc1_bias,
            w_fc1,
            first,
            w_fc2,
            second,
            i,
            tuple(sums),
            *((seqs, tensor_size) if i == halves - 1 else (1, 1)),
        )
        fed_parts.append((hidden, pre_grad, order.mark(pre_sum)))
        return sums

    def group(part):
        return Reduction(order, ((normed, part[1]), (grad, part[0])), block)

    def attend_next(row):
        result = attend(context_s, [order(row[0])] + list(row[1:]), direct)
        order.mark(result[0])
        if direct:
            back.append(send_across(*result))
        else:
            back.append([result[0]] + [to_context(result[m], m) for m in range(1, size)])

    waited = order.wait(*first_near[0], *second_near[0], *first_near[1:])
    first, second = list(waited[:across]), list(waited[across : 2 * across])
    first_near[1:] = waited[2 * across :]
    for i in range(1, halves):
        second_near.append(to_fsdp(after(second_mine[i], first_near[i])))
    sums = feed_part(0, to_both(first), to_both(second), sums)
    if direct:
        row = pass_on(*here[0])
        for own, beside, across_pair in pieces[1:]:
            here.append(send_across(own, beside, order(across_pair)))
    else:
        row = here[0]
    for i in range(1, halves):
        first, second = order.wait(first_near[i], second_near[i])
        sums = feed_part(i, to_both([first]), to_both([second]), sums)
    first_sum = group(fed_parts[0])
    second_sum = group(fed_parts[1])
    fed, fed_back = sums
    next_rows = [pass_on(*later) for later in here[1:]]
    fed_share = lax.psum_scatter(order(fed), "tensor", scatter_dimension=0, tiled=True)
    attend_next(row)
    for row in next_rows:
        attend_next(row)
    if not direct:
        stacked = jnp.stack(back[0])
        sources = lax.iota(jnp.int32, size) ^ context
        ordered = jnp.take(stacked, sources, axis=0)
        ordered = ordered.reshape(seq_groups, head_groups, seqs // seq_groups, 4, length, span)
        ordered = jnp.transpose(ordered, (0, 2, 3, 4, 1, 5))
        ordered = ordered.reshape(seqs, 4, length, heads_width)
        back = [[ordered[s : s + 1]] for s in range(seqs)]

    share = rows // tensor_size

    def turn_back(s, unturned):
        row = [order(back[s][0])] + back[s][1:]
        results = unturn(context_s, row, tables, s, rows, tuple(unturned))
        order.mark(results[0])
        return results

    def add_heads(s, raw_grad, norm_terms):
        return order.mark(
            norm_back(
                place_s,
                order(raw_grad),
                fed_back,
                w_qkv,
                rest_qkv,
                s,
                seqs,
                tensor_size,
                tuple(norm_terms),
            )
        )

    part_rows = length // tensor_size

    def heads_of(s, merged):
        def rows_for(mask):
            start = s * length + (tensor ^ mask) * part_rows
            return lax.dynamic_slice_in_dim(merged, start, part_rows, 0)

        return [rows_for(0)] + [to_tensor(rows_for(m), m) for m in range(1, tensor_size)]

    def arrived(*values):
        return order.wait(*values)

    if direct:
        back[0] = pass_on(*back[0])
    first_sum.send()
    unturned = []
    norm_terms = ()
    heads_from = []
    qkv_bias_sum = 0.0
    for s in range(seqs):
        *unturned, part_sum = turn_back(s, unturned)
        qkv_bias_sum = qkv_bias_sum + part_sum
        heads_from.append(heads_of(s, unturned[0]))
        norm_terms = [add_heads(s, unturned[1], norm_terms)]
        if direct and s + 1 < seqs:
            back[s + 1] = pass_on(*back[s + 1])
    merged, raw_grad = unturned
    last_sum = Reduction(order, ((grad, merged), (normed, raw_grad)), block)
    arrivals = arrived(*[piece for pieces_here in heads_from for piece in pieces_here[1:]])
    norm_share = order(norm_terms[0]).reshape(rows, width)
    norm_share = lax.psum_scatter(norm_share, "tensor", scatter_dimension=0, tiled=True)
    first_sum.keep()
    first_sum.over_fsdp(0)
    second_sum.send()
    last_sum.send()
    (first_sum.far[0],) = arrived(first_sum.far[0])
    first_sum.over_fsdp(1, first_sum.far[0])
    first_sum.over_chips(0)

    def in_order(blocks):
        return jnp.concatenate(own_blocks(blocks, 1, me, block), 1).astype(F32)

    def shared_rows(value):
        return lax.dynamic_slice_in_dim(value, tensor * part_rows, part_rows, 1).reshape(share, width)

    def from_shares(value):
        value = value.reshape(tensor_size, seqs, part_rows, width)
        return jnp.swapaxes(value, 0, 1).reshape(tokens.shape)

    inputs = shared_rows(tokens).astype(F32)
    all_heads = jnp.zeros((share, tensor_size * heads_width), BF16)
    arrivals = list(arrivals)
    for s in range(seqs):
        for m in range(tensor_size):
            piece = arrivals.pop(0) if m else heads_from[s][0]
            all_heads = lax.dynamic_update_slice(
                all_heads, order(piece), (s * part_rows, (tensor ^ m) * heads_width)
            )
    far = to_context(near, 1)
    near_part, far_part = nn(all_heads, near), nn(all_heads, far)
    attended = [near_part[:, :half], far_part[:, :half], near_part[:, half:], far_part[:, half:]]
    branch_sum = in_order(jnp.concatenate(attended, 1) + fed_share.astype(F32))
    block_out = (inputs + branch_sum + out_bias + fc2_bias).astype(BF16)
    order.mark(block_out)
    block_out = from_shares(lax.all_gather(block_out, "tensor", axis=0, tiled=True))
    second_sum.keep()
    first_sum.far[1], first_sum.far[0] = arrived(first_sum.far[1], first_sum.far[0])
    second_sum.over_fsdp(0, first_sum.far[1])
    first_sum.over_chips(1)
    first_sum.over_cores(0)
    last_sum.keep()

    normed_grad = in_order(order(norm_share))
    centered = inputs - jnp.mean(inputs, -1, keepdims=True)
    root = lax.rsqrt(jnp.mean(centered * centered, -1, keepdims=True) + EPSILON)
    unit = centered * root
    scaled = normed_grad * gain
    inner = jnp.mean(scaled * unit, -1, keepdims=True)
    input_part = root * (scaled - jnp.mean(scaled, -1, keepdims=True) - unit * inner)
    grad_share = shared_rows(cotangent).astype(F32)
    tokens_grad = (grad_share + input_part).astype(BF16)
    norm_sums = jnp.stack([jnp.sum(normed_grad * unit, 0), jnp.sum(normed_grad, 0)])
    order.mark(norm_sums)
    order.mark(tokens_grad)
    small_sums = [norm_sums.reshape(1, -1), bias_sum] + [part[2] for part in fed_parts]
    small_sums = jnp.concatenate(small_sums + [qkv_bias_sum], 1)
    small_other = to_context(small_sums, 1)
    second_sum.far[0], first_sum.far[1] = arrived(second_sum.far[0], first_sum.far[1])
    second_sum.over_fsdp(1, second_sum.far[0])
    second_sum.over_chips(0)
    first_sum.over_cores(1)
    second_sum.far[1], second_sum.far[0], small_other = arrived(
        second_sum.far[1], second_sum.far[0], small_other
    )
    small_sums = small_sums + small_other
    small_other = to_fsdp(small_sums)
    last_sum.over_fsdp(1, second_sum.far[1])
    second_sum.over_chips(1)
    second_sum.over_cores(0)
    small_sums = small_sums + order.wait(small_other)[0]
    for mask in masks_of(across):
        small_sums = small_sums + to_context(small_sums, 2 * mask)
    norm_sums = order.mark(small_sums)[0, : 2 * width].reshape(2, width)
    high = norm_sums.astype(BF16)
    low = (norm_sums - high.astype(F32)).astype(BF16)
    extra = jnp.concatenate([high, low, jnp.zeros((12, width), BF16)], 0)
    gathered = jnp.concatenate([order(tokens_grad), extra], 0)
    gathered = lax.all_gather(gathered, "tensor", axis=0, tiled=False)
    tokens_grad = from_shares(gathered[:, :share])
    norm_sums = jnp.sum(gathered[:, share : share + 4].astype(F32), 0)
    norm_sums = norm_sums[:2] + norm_sums[2:]
    fc1_grad = order.mark(
        finish(place_s, [first_sum.pieces[0], second_sum.pieces[0]], block)
    )
    last_sum.far[1], second_sum.far[1] = arrived(last_sum.far[1], second_sum.far[1])
    last_sum.over_fsdp(0, last_sum.far[1])
    last_sum.over_chips(1)
    second_sum.over_cores(1)
    fc2_grad = order.mark(
        finish(place_s, [first_sum.pieces[1], second_sum.pieces[1]], block, turned=True)
    )
    (last_sum.far[0],) = arrived(last_sum.far[0])
    last_sum.over_chips(0)
    last_sum.over_cores(1)
    qkv_grad = order.mark(finish(place_s, [last_sum.pieces[1]], block, groups=3))
    last_sum.over_cores(0)
    out_grad = order.mark(finish(place_s, [last_sum.pieces[0]], block, turned=True))
    units_here = b_fc1.shape[0] * 2
    small_sums = small_sums[0]
    other_sums = small_sums[2 * width :]

    def shard_of(value):
        part = value.shape[-1] // 2
        return lax.dynamic_slice_in_dim(value, shard * part, part, value.ndim - 1)

    out_bias_grad = shard_of(other_sums[:width])
    fc1_bias_grad = shard_of(other_sums[width : width + units_here])
    qkv_bias_grad = shard_of(other_sums[width + units_here :].reshape(3, heads_width))
    return (
        block_out,
        tokens_grad,
        shard_of(norm_sums[0]),
        shard_of(norm_sums[1]),
        qkv_grad,
        qkv_bias_grad,
        out_grad,
        out_bias_grad,
        fc1_grad,
        fc1_bias_grad,
        fc2_grad,
        out_bias_grad,
    )


def solution(mesh):
    return jax.shard_map(
        per_device,
        mesh=mesh,
        in_specs=(
            P("fsdp", "context", None),
            P("fsdp"),
            P("fsdp"),
            P(None, "fsdp", "tensor"),
            P(None, ("tensor", "fsdp")),
            P("tensor", "fsdp"),
            P("fsdp"),
            P("fsdp", "tensor"),
            P(("tensor", "fsdp")),
            P("tensor", "fsdp"),
            P("fsdp"),
            P("fsdp", "context", None),
        ),
        out_specs=(
            P("fsdp", "context", None),
            P("fsdp", "context", None),
            P("fsdp"),
            P("fsdp"),
            P(None, "fsdp", "tensor"),
            P(None, ("tensor", "fsdp")),
            P("tensor", "fsdp"),
            P("fsdp"),
            P("fsdp", "tensor"),
            P(("tensor", "fsdp")),
            P("tensor", "fsdp"),
            P("fsdp"),
        ),
        check_vma=False,
    )
```

```python
import functools

import jax
import jax.numpy as jnp
from jax import lax
import jax.experimental.pallas as pl
import jax.experimental.pallas.tpu as pltpu
from jax.sharding import PartitionSpec as P

HD = 64
ROT = 32
EPSILON = 1e-05
LANES = 128
F32 = jnp.float32
BF16 = jnp.bfloat16
ROOT = 0.7978845608028654
CUBE = 0.044715
VMEM_BYTES = 60 << 20


def lasting(micros):
    return pl.CostEstimate(flops=0, bytes_accessed=int(micros * 3.4e6), transcendentals=0)


def nn(a, b):
    return lax.dot_general(a, b, (((1,), (0,)), ((), ())), preferred_element_type=F32)


def nt(a, b):
    return lax.dot_general(a, b, (((1,), (1,)), ((), ())), preferred_element_type=F32)


def tn(a, b):
    return lax.dot_general(a, b, (((0,), (0,)), ((), ())), preferred_element_type=F32)


def add_low(*terms):
    total = terms[0].astype(F32)
    for term in terms[1:]:
        total = total + term.astype(F32)
    return total.astype(BF16)


def to_fsdp(value):
    return lax.ppermute(value, "fsdp", [(0, 1), (1, 0)])


def to_context(value, mask):
    size = lax.axis_size("context")
    return lax.ppermute(value, "context", [(i, i ^ mask) for i in range(size)])


def to_tensor(value, mask):
    size = lax.axis_size("tensor")
    return lax.ppermute(value, "tensor", [(i, i ^ mask) for i in range(size)])


def after(value, *others):
    return lax.optimization_barrier((value,) + others)[0]


def masks_of(size):
    mask = 1
    while mask < size:
        yield mask
        mask *= 2


def own_blocks(own, axis, place, block):
    count = own.shape[axis] // block
    return [
        lax.dynamic_slice_in_dim(own, (p ^ place) * block, block, axis) for p in range(count)
    ]


class Order:
    def __init__(self):
        self.last = None

    def __call__(self, value):
        return value if self.last is None else after(value, self.last)

    def mark(self, value):
        self.last = value
        return value

    def wait(self, *values):
        if self.last is not None:
            values = lax.optimization_barrier(values + (self.last,))[:-1]
        else:
            values = lax.optimization_barrier(values)
        self.last = values[0]
        return values


class Reduction:
    def __init__(self, order, pairs, block):
        self.order, self.pairs, self.block = order, pairs, block

    def compute(self):
        (self.sent,) = outer(self.order, self.pairs, 1, None)

    def send(self):
        self.compute()
        self.sent = to_context(self.sent, 1)

    def keep(self):
        results = outer(self.order, self.pairs, 0, self.sent)
        self.near, self.far = results[: len(self.pairs)], results[len(self.pairs) :]
        self.near, self.far = list(self.near), list(self.far)
        self.pieces = [None] * len(self.pairs)

    def over_fsdp(self, i, *earlier):
        self.far[i] = to_fsdp(after(self.far[i], *earlier) if earlier else self.far[i])
        return self.far[i]

    def over_chips(self, i):
        self.near[i] = self.order.mark(add_low(self.order(self.near[i]), self.far[i]))
        self.masks = list(masks_of(lax.axis_size("context") // 2))
        if self.masks:
            self.far[i] = to_context(self.near[i], 2 * self.masks[0])
        return self.far[i]

    def over_cores(self, i):
        total = self.near[i]
        for n, mask in enumerate(self.masks):
            other = self.far[i] if n == 0 else to_context(total, 2 * mask)
            total = self.order.mark(add_turned(self.order(total), other, mask, self.block))
        self.pieces[i] = (total, to_context(total, 1))


def prepare_kernel(count, me_ref, tokens, grad, gain, bias, normed_out, grad_out, sum_out, kept):
    values = tokens[...].astype(F32)
    centered = values - jnp.mean(values, -1, keepdims=True)
    variance = jnp.mean(centered * centered, -1, keepdims=True)
    kept[...] = (centered * lax.rsqrt(variance + EPSILON) * gain[...] + bias[...]).astype(BF16)
    me = me_ref[0]
    block = tokens.shape[1] // count
    for p in range(count):
        source = pl.ds(pl.multiple_of((p ^ me) * block, block), block)
        normed_out[:, p * block : (p + 1) * block] = kept[:, source]
        grad_out[:, p * block : (p + 1) * block] = grad[:, source]
    part = jnp.sum(grad[...].astype(F32), 0, keepdims=True)

    @pl.when(pl.program_id(0) == 0)
    def _():
        sum_out[...] = part

    @pl.when(pl.program_id(0) > 0)
    def _():
        sum_out[...] += part


def prepare(me, count, tokens, grad, gain, bias):
    rows, width = tokens.shape
    tile = min(128, rows)
    row_spec = pl.BlockSpec((tile, width), lambda r, me: (r, 0))
    one_spec = pl.BlockSpec((1, width), lambda r, me: (0, 0))
    return pl.pallas_call(
        functools.partial(prepare_kernel, count),
        out_shape=[
            jax.ShapeDtypeStruct((rows, width), BF16),
            jax.ShapeDtypeStruct((rows, width), BF16),
            jax.ShapeDtypeStruct((1, width), F32),
        ],
        grid_spec=pltpu.PrefetchScalarGridSpec(
            num_scalar_prefetch=1,
            grid=(rows // tile,),
            in_specs=[row_spec, row_spec, one_spec, one_spec],
            out_specs=[row_spec, row_spec, one_spec],
            scratch_shapes=[pltpu.VMEM((tile, width), BF16)],
        ),
        compiler_params=pltpu.CompilerParams(vmem_limit_bytes=VMEM_BYTES),
        cost_estimate=lasting(10),
        name="prepare",
    )(me, tokens, grad, gain, bias)


def turn(part, cosine, below, above):
    return (
        part * cosine
        + pltpu.roll(part, LANES - ROT // 2, 1) * below
        + pltpu.roll(part, ROT // 2, 1) * above
    )


def project_kernel(seqs, qkv_count, out_count, parts, k_ref, c_ref, *refs):
    normed, grad, bias, cosine, below, above = refs[:6]
    ends = (6 + qkv_count, 6 + qkv_count + out_count)
    outs, kept = refs[ends[1] : -1], refs[-1]
    which = pl.program_id(0)
    rows, width = kept.shape
    length = rows // seqs

    @pl.when(which < 3)
    def _():
        weight = jnp.concatenate([w[0] for w in refs[6 : ends[0]]], 0)
        raw = nn(normed[...], weight) + bias[0]

        @pl.when(which < 2)
        def _():
            for s in range(seqs):
                for lane in range(0, width, LANES):
                    part = raw[s * length : (s + 1) * length, lane : lane + LANES]
                    kept[s * length : (s + 1) * length, lane : lane + LANES] = turn(
                        part, cosine[...], below[...], above[...]
                    ).astype(BF16)

        @pl.when(which == 2)
        def _():
            kept[...] = raw.astype(BF16)

    @pl.when(which == 3)
    def _():
        weight = jnp.concatenate([w[...] for w in refs[ends[0] : ends[1]]], 1)
        kept[...] = nt(grad[...], weight).astype(BF16)

    span = width // parts
    for m in range(parts):
        at = pl.ds(pl.multiple_of((m ^ c_ref[0]) * span, span), span) if parts > 1 else slice(None)
        for s in range(seqs):
            part = kept[s * length : (s + 1) * length, at]
            if parts == 1:
                outs[s][0, 0] = part
            else:
                outs[3 * s + min(m, 2)][max(m - 2, 0), 0] = part


def project(place, context, normed, grad, qkv, qkv_rest, out, out_rest, bias, tables, seqs, parts):
    rows, depth = normed.shape
    width = qkv.shape[2]
    block = qkv_rest[0].shape[1]
    count = qkv.shape[1] // block
    length = rows // seqs
    span = width // parts
    table = pl.BlockSpec((length, LANES), lambda c, k, x: (0, 0))
    whole = pl.BlockSpec((rows, depth), lambda c, k, x: (0, 0), pipeline_mode=pl.Buffered(1))

    def qkv_spec(p):
        return pl.BlockSpec((1, block, width), lambda c, k, x: (jnp.minimum(c, 2), p ^ k[0], 0))

    def out_spec(p):
        return pl.BlockSpec((width, block), lambda c, k, x: (0, p ^ k[0]))

    qkv_specs = [qkv_spec(p) for p in range(count)] + [
        pl.BlockSpec((1, block, width), lambda c, k, x: (jnp.minimum(c, 2), 0, 0))
    ] * len(qkv_rest)
    out_specs = [out_spec(p) for p in range(count)] + [
        pl.BlockSpec((width, block), lambda c, k, x: (0, 0))
    ] * len(out_rest)
    counts = [1] if parts == 1 else [1, 1, 2]
    results = pl.pallas_call(
        functools.partial(project_kernel, seqs, len(qkv_specs), len(out_specs), parts),
        out_shape=[jax.ShapeDtypeStruct((n, 4, length, span), BF16) for n in counts] * seqs,
        grid_spec=pltpu.PrefetchScalarGridSpec(
            num_scalar_prefetch=2,
            grid=(4,),
            in_specs=[
                whole,
                whole,
                pl.BlockSpec((1, 1, width), lambda c, k, x: (jnp.minimum(c, 2), 0, 0)),
                table,
                table,
                table,
            ]
            + qkv_specs
            + out_specs,
            out_specs=[
                pl.BlockSpec((n, 1, length, span), lambda c, k, x: (0, c, 0, 0)) for n in counts
            ]
            * seqs,
            scratch_shapes=[pltpu.VMEM((rows, width), BF16)],
        ),
        compiler_params=pltpu.CompilerParams(vmem_limit_bytes=VMEM_BYTES),
        cost_estimate=lasting(19),
        name="project",
    )(
        place,
        context,
        normed,
        grad,
        bias,
        *tables,
        *([qkv] * count),
        *qkv_rest,
        *([out] * count),
        *out_rest,
    )
    return [results[s * len(counts) : (s + 1) * len(counts)] for s in range(seqs)]


def attend_kernel(parts, bq, bk, me_ref, *refs):
    pieces = refs[:parts]
    outs = refs[parts:-11]
    q_all, k_all, v_all, g_all, v_turned, k_turned, o_all, dq_all, dk_all, dv_all, held = refs[-11:]
    rows, width = pieces[0].shape[2:]
    length = rows * parts
    me = me_ref[0]
    scale = HD**-0.5
    for m in range(parts):
        at = pl.ds(pl.multiple_of((me ^ m) * rows, rows), rows)
        q_all[at, :] = (pieces[m][0, 0].astype(F32) * scale).astype(BF16)
        k_all[at, :] = pieces[m][0, 1]
        v_all[at, :] = pieces[m][0, 2]
        g_all[at, :] = pieces[m][0, 3]
    v_turned[...] = v_all[...].T
    k_turned[...] = k_all[...].T
    dk_all[...] = jnp.zeros_like(dk_all)
    dv_all[...] = jnp.zeros_like(dv_all)
    heads = width // HD
    lane_head = lax.broadcasted_iota(jnp.int32, (1, width), 1) // HD

    for first in range(0, length, bq):
        at_q = slice(first, first + bq)
        query, grad = q_all[at_q, :], g_all[at_q, :]
        spans = [slice(k, min(k + bk, first + bq)) for k in range(0, first + bq, bk)]
        outputs, q_grads = [], []
        for h in range(heads):
            at_h = slice(h * HD, (h + 1) * HD)
            q_head = jnp.where(lane_head == h, query, jnp.zeros_like(query))
            g_head = jnp.where(lane_head == h, grad, jnp.zeros_like(grad))
            top = jnp.full((8, bq), -1e30, F32)
            for span in spans:
                scores = nt(k_all[span, :], q_head)
                free = min(span.stop, max(first, span.start)) - span.start
                if free:
                    part = scores[:free]
                    held[span.start : span.start + free, :] = part
                    top = jnp.maximum(top, jnp.max(part.reshape(free // 8, 8, bq), 0))
                rest = span.stop - span.start - free
                if rest:
                    key = span.start + free + lax.broadcasted_iota(jnp.int32, (rest, bq), 0)
                    place = first + lax.broadcasted_iota(jnp.int32, (rest, bq), 1)
                    part = jnp.where(key <= place, scores[free:], -1e30)
                    held[span.start + free : span.stop, :] = part
                    top = jnp.maximum(top, jnp.max(part.reshape(rest // 8, 8, bq), 0))
            top = jnp.max(top, 0, keepdims=True)
            total = jnp.zeros((8, bq), F32)
            output = jnp.zeros((HD, bq), F32)
            for span in spans:
                weights = jnp.exp(held[span, :] - top)
                held[span, :] = weights
                total = total + jnp.sum(weights.reshape(-1, 8, bq), 0)
                output = output + nn(v_turned[at_h, span], weights.astype(BF16))
            inverse = 1.0 / jnp.sum(total, 0, keepdims=True)
            output = output * inverse
            g_turned = g_head.T.astype(F32)
            inner = jnp.sum(output * g_turned[at_h], 0, keepdims=True) * inverse
            g_scaled = (g_turned * inverse).astype(BF16)
            g_rows = g_scaled.T
            q_grad = jnp.zeros((HD, bq), F32)
            for span in spans:
                weights = held[span, :]
                prob_grad = nn(v_all[span, :], g_scaled)
                score_grad = (weights * (prob_grad - inner)).astype(BF16)
                dv_all[span, :] += nn(weights.astype(BF16), g_rows)
                dk_all[span, :] += nn(score_grad, q_head)
                q_grad = q_grad + nn(k_turned[at_h, span], score_grad)
            outputs.append(output)
            q_grads.append(q_grad * scale)
        o_all[at_q, :] = jnp.concatenate(outputs, 0).T.astype(BF16)
        dq_all[at_q, :] = jnp.concatenate(q_grads, 0).T.astype(BF16)
    for m in range(parts):
        at = pl.ds(pl.multiple_of((me ^ m) * rows, rows), rows)
        out, i = (outs[m], 0) if len(outs) == parts else (outs[min(m, 2)], max(m - 2, 0))
        out[i, 0] = o_all[at, :]
        out[i, 1] = dq_all[at, :]
        out[i, 2] = dk_all[at, :].astype(BF16)
        out[i, 3] = dv_all[at, :].astype(BF16)


def attend(context, pieces, paired):
    parts = len(pieces)
    seqs, _, rows, width = pieces[0].shape
    length = rows * parts
    bq = min(512, length)
    bk = min(2048, length)
    vmem = pltpu.VMEM
    counts = [1, 1, 2] if paired else [seqs] * parts
    return pl.pallas_call(
        functools.partial(attend_kernel, parts, bq, bk),
        out_shape=[jax.ShapeDtypeStruct((n, 4, rows, width), BF16) for n in counts],
        grid_spec=pltpu.PrefetchScalarGridSpec(
            num_scalar_prefetch=1,
            grid=(seqs,),
            in_specs=[pl.BlockSpec((1, 4, rows, width), lambda s, me: (s, 0, 0, 0))] * parts,
            out_specs=[
                pl.BlockSpec((n if paired else 1, 4, rows, width), lambda s, me: (s, 0, 0, 0))
                for n in counts
            ],
            scratch_shapes=[vmem((length, width), BF16)] * 4
            + [vmem((width, length), BF16)] * 2
            + [vmem((length, width), BF16)] * 2
            + [vmem((length, width), F32)] * 2
            + [vmem((length, bq), F32)],
        ),
        compiler_params=pltpu.CompilerParams(vmem_limit_bytes=VMEM_BYTES),
        cost_estimate=lasting(28),
        name="attend",
    )(context, *pieces)


def unturn_kernel(parts, c_ref, *refs):
    pieces = refs[:parts]
    cosine, below, above = refs[parts : parts + 3]
    merged, raw, sums = refs[-3:]
    width = merged.shape[1]
    span = width // parts
    for m in range(parts):
        at = pl.ds(pl.multiple_of((m ^ c_ref[0]) * span, span), span) if parts > 1 else slice(None)
        merged[:, at] = pieces[m][0, 0]
    for c in range(3):
        for m in range(parts):
            for lane in range(0, span, LANES):
                start = (m ^ c_ref[0]) * span + c * width + lane if parts > 1 else c * width + lane
                at = pl.ds(pl.multiple_of(start, LANES), LANES)
                part = pieces[m][0, c + 1, :, lane : lane + LANES]
                if c < 2:
                    part = turn(part.astype(F32), cosine[...], -below[...], -above[...])
                    part = part.astype(BF16)
                raw[:, at] = part
                sums[:, at] = jnp.sum(part.astype(F32), 0, keepdims=True)


def unturn(context, pieces, tables, s, rows, earlier):
    parts = len(pieces)
    length, span = pieces[0].shape[2:]
    width = span * parts
    vmem = pl.BlockSpec(memory_space=pltpu.VMEM)
    return pl.pallas_call(
        functools.partial(unturn_kernel, parts),
        out_shape=[
            jax.ShapeDtypeStruct((rows, width), BF16),
            jax.ShapeDtypeStruct((rows, 3 * width), BF16),
            jax.ShapeDtypeStruct((1, 3 * width), F32),
        ],
        grid=(1,),
        in_specs=[pl.BlockSpec(memory_space=pltpu.SMEM)]
        + [vmem] * (parts + 3)
        + [pl.BlockSpec(memory_space=pl.ANY)] * len(earlier),
        out_specs=[
            pl.BlockSpec((length, width), lambda i: (s, 0)),
            pl.BlockSpec((length, 3 * width), lambda i: (s, 0)),
            vmem,
        ],
        input_output_aliases={parts + 4 + i: i for i in range(len(earlier))},
        compiler_params=pltpu.CompilerParams(vmem_limit_bytes=VMEM_BYTES),
        cost_estimate=lasting(4),
        name="unturn",
    )(context, *pieces, *tables, *earlier)


def norm_back_kernel(count, k_ref, raw, back, *refs):
    out, total = refs[-2:]
    weight = jnp.concatenate([w[0] for w in refs[:count]], 0)
    term = nt(raw[...], weight)
    step = pl.program_id(0)

    @pl.when(step == 0)
    def _():
        total[...] = back[...].astype(F32) + term

    @pl.when(step == 1)
    def _():
        total[...] += term

    @pl.when(step == 2)
    def _():
        out[...] = (total[...] + term).astype(BF16).reshape(out.shape)


def norm_back(place, raw, back, own, rest, s, seqs, shares, earlier):
    rows, depth = back.shape
    width = own.shape[2]
    block = rest[0].shape[1]
    count = own.shape[1] // block
    length = rows // seqs

    def own_spec(p):
        return pl.BlockSpec((1, block, width), lambda c, k: (c, p ^ k[0], 0))

    specs = [own_spec(p) for p in range(count)] + [
        pl.BlockSpec((1, block, width), lambda c, k: (c, 0, 0))
    ] * len(rest)
    return pl.pallas_call(
        functools.partial(norm_back_kernel, len(specs)),
        out_shape=jax.ShapeDtypeStruct((shares, seqs, length // shares, depth), BF16),
        grid_spec=pltpu.PrefetchScalarGridSpec(
            num_scalar_prefetch=1,
            grid=(3,),
            in_specs=[
                pl.BlockSpec((length, width), lambda c, k: (s, c)),
                pl.BlockSpec((length, depth), lambda c, k: (s, 0)),
            ]
            + specs
            + [pl.BlockSpec(memory_space=pl.ANY)] * len(earlier),
            out_specs=pl.BlockSpec(
                (shares, 1, length // shares, depth), lambda c, k: (0, s, 0, 0)
            ),
            scratch_shapes=[pltpu.VMEM((length, depth), F32)],
        ),
        input_output_aliases={3 + len(specs) + i: i for i in range(len(earlier))},
        compiler_params=pltpu.CompilerParams(vmem_limit_bytes=VMEM_BYTES),
        cost_estimate=lasting(8),
        name="norm_back",
    )(place, raw, back, *([own] * count), *rest, *earlier)


def gelu_pair(value):
    square = value * value
    bent = jnp.tanh(ROOT * value * (1.0 + CUBE * square))
    half = 0.5 * (1.0 + bent)
    slope = half + 0.5 * value * (1.0 - bent * bent) * (ROOT * (1.0 + 3.0 * CUBE * square))
    return value * half, slope


def feed_kernel(first_count, second_count, onto, seqs, shares, k_ref, *refs):
    normed, grad, bias = refs[:3]
    ends = (3 + first_count, 3 + first_count + second_count)
    first = jnp.concatenate([r[...] for r in refs[3 : ends[0]]], 0)
    second = jnp.concatenate([r[...] for r in refs[ends[0] : ends[1]]], 1)
    hidden_out, pre_grad_out, sum_out, fed_out, back_out, fed, back = refs[ends[1] + onto :]
    tile = pl.program_id(0)

    hidden, slope = gelu_pair(nn(normed[...], first) + bias[...])
    hidden_low = hidden.astype(BF16)
    pre_grad = (nt(grad[...], second) * slope).astype(BF16)
    hidden_out[...] = hidden_low
    pre_grad_out[...] = pre_grad

    @pl.when(tile == 0)
    def _():
        fed[...] = nn(hidden_low, second)
        back[...] = nt(pre_grad, first)

    @pl.when(tile > 0)
    def _():
        fed[...] += nn(hidden_low, second)
        back[...] += nt(pre_grad, first)

    if onto:
        some = refs[ends[1]].shape[0]
        at = pl.ds(pl.multiple_of(tile * some, some), some)
        fed[at, :] += refs[ends[1]][...].astype(F32)
        back[at, :] += refs[ends[1] + 1][...].astype(F32)
    sum_out[...] = jnp.sum(pre_grad.astype(F32), 0, keepdims=True)

    @pl.when(tile == pl.num_programs(0) - 1)
    def _():
        tile_rows = fed.shape[0] // (seqs * shares)
        for to in range(seqs * shares):
            source = (to % seqs * shares + to // seqs) * tile_rows
            fed_out[to * tile_rows : (to + 1) * tile_rows, :] = fed[
                source : source + tile_rows, :
            ].astype(BF16)
        back_out[...] = back[...].astype(BF16)


def feed(
    place,
    block,
    normed,
    grad,
    bias,
    own_first,
    rest_first,
    own_second,
    rest_second,
    part,
    sums,
    seqs,
    shares,
):
    rows, width = normed.shape
    inside = rest_first[0].shape[0] // block
    units = rest_first[0].shape[1]
    count = own_first.shape[0] // block
    tile = min(512, units)
    skip = part * (units // tile)
    whole = pl.BlockSpec((rows, width), lambda t, k: (0, 0), pipeline_mode=pl.Buffered(1))

    def first_spec(p):
        return pl.BlockSpec((block, tile), lambda t, k: (p ^ k[0], t + skip))

    def second_spec(p):
        return pl.BlockSpec((tile, block), lambda t, k: (t + skip, p ^ k[0]))

    def first_rest(p):
        return pl.BlockSpec((block, tile), lambda t, k: (p ^ (k[0] % inside), t))

    def second_rest(p):
        return pl.BlockSpec((tile, block), lambda t, k: (t, p ^ (k[0] % inside)))

    first = [first_spec(p) for p in range(count)]
    first += [first_rest(p) for p in range(inside)] * len(rest_first)
    second = [second_spec(p) for p in range(count)]
    second += [second_rest(p) for p in range(inside)] * len(rest_second)
    unit_rows = pl.BlockSpec((rows, tile), lambda t, k: (0, t))
    return pl.pallas_call(
        functools.partial(feed_kernel, len(first), len(second), len(sums), seqs, shares),
        out_shape=[
            jax.ShapeDtypeStruct((rows, units), BF16),
            jax.ShapeDtypeStruct((rows, units), BF16),
            jax.ShapeDtypeStruct((1, units), F32),
            jax.ShapeDtypeStruct((rows, width), BF16),
            jax.ShapeDtypeStruct((rows, width), BF16),
        ],
        grid_spec=pltpu.PrefetchScalarGridSpec(
            num_scalar_prefetch=1,
            grid=(units // tile,),
            in_specs=[whole, whole, pl.BlockSpec((1, tile), lambda t, k: (0, t + skip))]
            + first
            + second
            + [pl.BlockSpec((rows // (units // tile), width), lambda t, k: (t, 0))] * len(sums),
            out_specs=[
                unit_rows,
                unit_rows,
                pl.BlockSpec((1, tile), lambda t, k: (0, t)),
                whole,
                whole,
            ],
            scratch_shapes=[pltpu.VMEM((rows, width), F32)] * 2,
        ),
        compiler_params=pltpu.CompilerParams(vmem_limit_bytes=VMEM_BYTES),
        cost_estimate=lasting(31),
        name="feed",
    )(
        place,
        normed,
        grad,
        bias,
        *([own_first] * count),
        *[piece for piece in rest_first for _ in range(inside)],
        *([own_second] * count),
        *[piece for piece in rest_second for _ in range(inside)],
        *sums,
    )


def outer_kernel(steps, adds, *refs):
    count = len(steps)
    lefts, rights = refs[: 2 * count], refs[2 * count : 3 * count]
    outs = refs[3 * count + adds : -1]
    turned = refs[-1]
    quarter = lefts[0].shape[1]
    step = pl.program_id(0)
    start = 0
    for i in range(count):

        @pl.when(step == start)
        def _():
            turned[:quarter, :] = lefts[2 * i][...].T
            turned[quarter:, :] = lefts[2 * i + 1][...].T

        @pl.when((step >= start) & (step < start + steps[i]))
        def _():
            value = nn(turned[...], rights[i][...])
            for high in range(2):
                part = value[high * quarter : (high + 1) * quarter]
                if adds:
                    part = part + refs[3 * count][high].astype(F32)
                    outs[high * count + i][...] = part.astype(BF16)
                else:
                    outs[0][high] = part.astype(BF16)

        start += steps[i]


def outer(order, pairs, low, received):
    rows, width = pairs[0][0].shape
    quarter = width // 4
    tile = min([512] + [right.shape[1] for _, right in pairs])
    steps = [right.shape[1] // tile for _, right in pairs]
    total = sum(steps) * tile
    adds = received is not None

    def left_spec(high):
        return pl.BlockSpec((rows, quarter), lambda t: (0, 2 * high + low))

    def column_spec(height, i):
        start = sum(steps[:i])
        return pl.BlockSpec((height, tile), lambda t: (0, jnp.clip(t - start, 0, steps[i] - 1)))

    both = pl.BlockSpec((2, quarter, tile), lambda t: (0, 0, t))
    if adds:
        out_shape = [
            jax.ShapeDtypeStruct((quarter, right.shape[1]), BF16) for _, right in pairs
        ] * 2
        out_specs = [column_spec(quarter, i) for i in range(len(pairs))] * 2
    else:
        out_shape = [jax.ShapeDtypeStruct((2, quarter, total), BF16)]
        out_specs = [both]
    results = pl.pallas_call(
        functools.partial(outer_kernel, steps, int(adds)),
        out_shape=out_shape,
        grid=(sum(steps),),
        in_specs=[left_spec(high) for _ in pairs for high in range(2)]
        + [column_spec(rows, i) for i in range(len(pairs))]
        + [both] * adds,
        out_specs=out_specs,
        scratch_shapes=[pltpu.VMEM((2 * quarter, rows), BF16)],
        compiler_params=pltpu.CompilerParams(vmem_limit_bytes=VMEM_BYTES),
        cost_estimate=lasting(11),
        name="outer",
    )(
        *[left for left, _ in pairs for _ in range(2)],
        *[order(right) if i == 0 else right for i, (_, right) in enumerate(pairs)],
        *([received] if adds else []),
    )
    order.mark(results[0])
    return results


def add_turned_kernel(left, right, out):
    out[...] = add_low(left[...], right[...])


def add_turned(left, right, mask, block):
    rows, width = left.shape
    tile = width
    spec = pl.BlockSpec((block, tile), lambda p, t: (p, t))
    return pl.pallas_call(
        add_turned_kernel,
        out_shape=jax.ShapeDtypeStruct((rows, width), BF16),
        grid=(rows // block, width // tile),
        in_specs=[spec, pl.BlockSpec((block, tile), lambda p, t: (p ^ mask, t))],
        out_specs=spec,
        cost_estimate=lasting(2.5),
        name="add_turned",
    )(left, right)


def finish_kernel(half, turned, groups, k_ref, *refs):
    out = refs[-1]
    pieces = refs[:-1]
    for i, piece in enumerate(pieces):
        width = piece.shape[1] // groups

        @pl.when(pl.program_id(0) // half == i % 2)
        def _():
            value = piece[...].astype(F32)
            start = i // 2 * piece.shape[1]
            if groups > 1:
                for g in range(groups):
                    out[g] = value[:, g * width : (g + 1) * width]
            elif turned:
                out[start : start + width, :] = value.T
            else:
                out[:, start : start + width] = value


def finish(place, parts, block, turned=False, groups=1):
    rows, some = parts[0][0].shape
    width = some * len(parts)
    half = rows // block
    if groups > 1:
        shape = (groups, 2 * rows, width // groups)
        out_spec = pl.BlockSpec((groups, block, width // groups), lambda p, k: (0, p ^ k[0], 0))
    elif turned:
        shape = (width, 2 * rows)
        out_spec = pl.BlockSpec((width, block), lambda p, k: (0, p ^ k[0]))
    else:
        shape = (2 * rows, width)
        out_spec = pl.BlockSpec((block, width), lambda p, k: (p ^ k[0], 0))

    def piece_spec(side):
        return pl.BlockSpec((block, some), lambda p, k: (jnp.clip(p - side * half, 0, half - 1), 0))

    return pl.pallas_call(
        functools.partial(finish_kernel, half, turned, groups),
        out_shape=jax.ShapeDtypeStruct(shape, F32),
        grid_spec=pltpu.PrefetchScalarGridSpec(
            num_scalar_prefetch=1,
            grid=(2 * half,),
            in_specs=[piece_spec(side) for _ in parts for side in (0, 1)],
            out_specs=out_spec,
        ),
        compiler_params=pltpu.CompilerParams(vmem_limit_bytes=VMEM_BYTES),
        cost_estimate=lasting(6),
        name="finish",
    )(place, *[piece for part in parts for piece in part])


def rotation_tables(positions):
    half = ROT // 2
    exponents = lax.iota(jnp.int32, half).astype(F32) * (2.0 / ROT)
    angles = positions[:, None] * jnp.power(10000.0, -exponents)[None, :]
    cosine, sine = jnp.cos(angles), jnp.sin(angles)
    ones = jnp.ones((positions.shape[0], HD - ROT), F32)
    none = jnp.zeros_like(ones)
    nought = jnp.zeros_like(sine)
    copies = LANES // HD
    return (
        jnp.concatenate([cosine, cosine, ones] * copies, 1),
        jnp.concatenate([-sine, nought, none] * copies, 1),
        jnp.concatenate([nought, sine, none] * copies, 1),
    )


def per_device(
    tokens, ln_gain, ln_bias, w_qkv, b_qkv, w_out, b_out, w_fc1, b_fc1, w_fc2, b_fc2, cotangent
):
    seqs, length, width = tokens.shape
    size = lax.axis_size("context")
    context = lax.axis_index("context")
    shard = lax.axis_index("fsdp")
    tensor_size = lax.axis_size("tensor")
    tensor = lax.axis_index("tensor")
    across = size // 2
    place = (context & 1) * across + context // 2
    me = shard * size + place
    block = width // (2 * size)
    rows = seqs * length
    heads_width = w_out.shape[0]
    heads_local = heads_width // HD
    head_groups = min(heads_local, size)
    seq_groups = size // head_groups
    span = heads_width // head_groups
    direct = seq_groups == 1 and span % LANES == 0 and size == 4
    me_s, place_s, context_s = (jnp.reshape(v, (1,)).astype(jnp.int32) for v in (me, place, context))

    small = (ln_gain, ln_bias, b_out, b_fc2, b_fc1, b_qkv.reshape(-1))
    packed = jnp.concatenate(small)
    other = to_fsdp(packed)
    halves = 2
    units = w_fc1.shape[1] // halves

    def qkv_at(p):
        return lax.dynamic_slice_in_dim(w_qkv, (place ^ p) * block, block, 1)

    def out_at(p):
        return lax.dynamic_slice_in_dim(w_out, (place ^ p) * block, block, 1)

    flat = tokens.reshape(rows, width)
    grad_flat = cotangent.reshape(rows, width)
    both = jnp.where(shard == 0, jnp.stack([packed, other]), jnp.stack([other, packed]))
    both = both.astype(F32)
    vectors = []
    at = 0
    for value in small:
        vectors.append(both[:, at : at + value.size])
        at += value.size
    gain, bias, out_bias, fc2_bias, fc1_bias = (v.reshape(1, -1) for v in vectors[:5])
    qkv_bias = jnp.swapaxes(vectors[5].reshape(2, 3, -1), 0, 1).reshape(3, 1, heads_width)
    normed, grad, bias_sum = prepare(me_s, 2 * size, flat, grad_flat, gain, bias)
    positions = (context * length + lax.iota(jnp.int32, length)).astype(F32)
    tables = rotation_tables(positions)
    bias_sum, *tables = lax.optimization_barrier((bias_sum, *tables))

    order = Order()
    half = across * block
    core = context & 1

    def fc_from(i, *done):
        first = lax.dynamic_slice(w_fc1, (core * half, i * units), (half, units))
        second = lax.dynamic_slice(w_fc2, (i * units, core * half), (units, half))
        return to_fsdp(after(first, *done)), to_fsdp(after(second, *done))

    first_mine = [
        lax.dynamic_slice(w_fc1, (core * half, i * units), (half, units)) for i in range(halves)
    ]
    second_mine = [
        lax.dynamic_slice(w_fc2, (i * units, core * half), (units, half)) for i in range(halves)
    ]
    def spread(pieces):
        for mask in masks_of(across):
            pieces = pieces + [to_context(piece, 2 * mask) for piece in pieces]
        return pieces

    def to_both(pieces):
        return pieces + [to_context(piece, 1) for piece in pieces]

    rest_qkv = [to_fsdp(qkv_at(0))]
    ready = rest_qkv[0]
    rest_out = [to_fsdp(after(out_at(0), ready))]
    first_block = lax.dynamic_slice(w_fc1, (place * block, 0), (block, units))
    second_block = lax.dynamic_slice(w_fc2, (0, place * block), (units, block))
    first_near = [[to_fsdp(after(first_block, ready))]]
    second_near = [[to_fsdp(after(second_block, ready))]]
    order.mark(bias_sum)
    rest_qkv = spread(rest_qkv)
    mine = first_mine[1:] + second_mine[1:]
    waited = order.wait(*rest_qkv, *rest_out, *mine)
    rest_qkv, rest_out = list(waited[:across]), list(waited[across : -len(mine)])
    first_mine[1:], second_mine[1:] = waited[-len(mine) : 1 - halves], waited[1 - halves :]
    rest_out = spread(rest_out)
    rest_qkv = to_both(rest_qkv)
    waited = order.wait(first_near[0][0], second_near[0][0], *rest_out)
    rest_out = to_both(list(waited[2:]))
    first_near[0], second_near[0] = spread([waited[0]]), spread([waited[1]])
    for i in range(1, halves):
        first_near.append(to_fsdp(after(first_mine[i], waited[1])))

    near = jnp.concatenate([out_at(p) for p in range(across)] + rest_out[:across], 1)
    near = lax.all_gather(near, "tensor", axis=0, tiled=True)

    pieces = project(
        place_s,
        context_s,
        order(normed),
        grad,
        w_qkv,
        rest_qkv,
        w_out,
        rest_out,
        qkv_bias,
        tables,
        seqs,
        size if direct else 1,
    )
    def send_across(own, beside, across_pair):
        return own, beside, to_context(across_pair, 2)

    def pass_on(own, beside, far_pair):
        (far_pair,) = order.wait(far_pair)
        return [own, to_context(order(beside), 1), far_pair[:1], to_context(far_pair[1:], 1)]

    if direct:
        here = [send_across(*pieces[0])]
    else:
        field = jnp.concatenate([row[0] for row in pieces], 0)

        def part_for(mask):
            target = context ^ mask
            starts = [0] * 4
            sizes = list(field.shape)
            starts[0] = (target // head_groups) * (seqs // seq_groups)
            sizes[0] = seqs // seq_groups
            starts[3] = (target % head_groups) * span
            sizes[3] = span
            return lax.dynamic_slice(field, starts, sizes)

        here = [[part_for(0)] + [to_context(part_for(m), m) for m in range(1, size)]]

    order.mark(pieces[0][0])

    sums = ()
    fed_parts = []
    back = []

    def feed_part(i, first, second, sums):
        hidden, pre_grad, pre_sum, *sums = feed(
            place_s,
            block,
            order(normed),
            grad,
            fc1_bias,
            w_fc1,
            first,
            w_fc2,
            second,
            i,
            tuple(sums),
            *((seqs, tensor_size) if i == halves - 1 else (1, 1)),
        )
        fed_parts.append((hidden, pre_grad, order.mark(pre_sum)))
        return sums

    def group(part):
        return Reduction(order, ((normed, part[1]), (grad, part[0])), block)

    def attend_next(row):
        result = attend(context_s, [order(row[0])] + list(row[1:]), direct)
        order.mark(result[0])
        if direct:
            back.append(send_across(*result))
        else:
            back.append([result[0]] + [to_context(result[m], m) for m in range(1, size)])

    waited = order.wait(*first_near[0], *second_near[0], *first_near[1:])
    first, second = list(waited[:across]), list(waited[across : 2 * across])
    first_near[1:] = waited[2 * across :]
    for i in range(1, halves):
        second_near.append(to_fsdp(after(second_mine[i], first_near[i])))
    sums = feed_part(0, to_both(first), to_both(second), sums)
    if direct:
        row = pass_on(*here[0])
        for own, beside, across_pair in pieces[1:]:
            here.append(send_across(own, beside, order(across_pair)))
    else:
        row = here[0]
    for i in range(1, halves):
        first, second = order.wait(first_near[i], second_near[i])
        row = list(order.wait(*row))
        sums = feed_part(i, to_both([first]), to_both([second]), sums)
    first_sum = group(fed_parts[0])
    second_sum = group(fed_parts[1])
    fed, fed_back = sums
    next_rows = [pass_on(*later) for later in here[1:]]
    fed_share = lax.psum_scatter(order(fed), "tensor", scatter_dimension=0, tiled=True)
    attend_next(row)
    for row in next_rows:
        attend_next(row)
    if not direct:
        stacked = jnp.stack(back[0])
        sources = lax.iota(jnp.int32, size) ^ context
        ordered = jnp.take(stacked, sources, axis=0)
        ordered = ordered.reshape(seq_groups, head_groups, seqs // seq_groups, 4, length, span)
        ordered = jnp.transpose(ordered, (0, 2, 3, 4, 1, 5))
        ordered = ordered.reshape(seqs, 4, length, heads_width)
        back = [[ordered[s : s + 1]] for s in range(seqs)]

    share = rows // tensor_size

    def turn_back(s, unturned):
        row = [order(back[s][0])] + back[s][1:]
        results = unturn(context_s, row, tables, s, rows, tuple(unturned))
        order.mark(results[0])
        return results

    def add_heads(s, raw_grad, norm_terms):
        return order.mark(
            norm_back(
                place_s,
                order(raw_grad),
                fed_back,
                w_qkv,
                rest_qkv,
                s,
                seqs,
                tensor_size,
                tuple(norm_terms),
            )
        )

    part_rows = length // tensor_size

    def heads_of(s, merged):
        def rows_for(mask):
            start = s * length + (tensor ^ mask) * part_rows
            return lax.dynamic_slice_in_dim(merged, start, part_rows, 0)

        return [rows_for(0)] + [to_tensor(rows_for(m), m) for m in range(1, tensor_size)]

    def arrived(*values):
        return order.wait(*values)

    if direct:
        back[0] = pass_on(*back[0])
    first_sum.compute()
    first_sum.sent = to_context(after(first_sum.sent, *back[0][1:]), 1)
    unturned = []
    norm_terms = ()
    heads_from = []
    qkv_bias_sum = 0.0
    for s in range(seqs):
        *unturned, part_sum = turn_back(s, unturned)
        qkv_bias_sum = qkv_bias_sum + part_sum
        heads_from.append(heads_of(s, unturned[0]))
        norm_terms = [add_heads(s, unturned[1], norm_terms)]
        if direct and s + 1 < seqs:
            back[s + 1] = pass_on(*back[s + 1])
    merged, raw_grad = unturned
    last_sum = Reduction(order, ((grad, merged), (normed, raw_grad)), block)
    arrivals = arrived(*[piece for pieces_here in heads_from for piece in pieces_here[1:]])
    norm_share = order(norm_terms[0]).reshape(rows, width)
    norm_share = lax.psum_scatter(norm_share, "tensor", scatter_dimension=0, tiled=True)
    first_sum.keep()
    first_sum.over_fsdp(0)
    second_sum.send()
    last_sum.send()
    (first_sum.far[0],) = arrived(first_sum.far[0])
    first_sum.over_fsdp(1, first_sum.far[0])
    first_sum.over_chips(0)

    def in_order(blocks):
        return jnp.concatenate(own_blocks(blocks, 1, me, block), 1).astype(F32)

    def shared_rows(value):
        return lax.dynamic_slice_in_dim(value, tensor * part_rows, part_rows, 1).reshape(share, width)

    def from_shares(value):
        value = value.reshape(tensor_size, seqs, part_rows, width)
        return jnp.swapaxes(value, 0, 1).reshape(tokens.shape)

    inputs = shared_rows(tokens).astype(F32)
    all_heads = jnp.zeros((share, tensor_size * heads_width), BF16)
    arrivals = list(arrivals)
    for s in range(seqs):
        for m in range(tensor_size):
            piece = arrivals.pop(0) if m else heads_from[s][0]
            all_heads = lax.dynamic_update_slice(
                all_heads, order(piece), (s * part_rows, (tensor ^ m) * heads_width)
            )
    far = to_context(near, 1)
    near_part, far_part = nn(all_heads, near), nn(all_heads, far)
    attended = [near_part[:, :half], far_part[:, :half], near_part[:, half:], far_part[:, half:]]
    branch_sum = in_order(jnp.concatenate(attended, 1) + fed_share.astype(F32))
    block_out = (inputs + branch_sum + out_bias + fc2_bias).astype(BF16)
    order.mark(block_out)
    block_out = from_shares(lax.all_gather(block_out, "tensor", axis=0, tiled=True))
    second_sum.keep()
    first_sum.far[1], first_sum.far[0] = arrived(first_sum.far[1], first_sum.far[0])
    second_sum.over_fsdp(0, first_sum.far[1])
    first_sum.over_chips(1)
    first_sum.over_cores(0)
    last_sum.keep()

    normed_grad = in_order(order(norm_share))
    centered = inputs - jnp.mean(inputs, -1, keepdims=True)
    root = lax.rsqrt(jnp.mean(centered * centered, -1, keepdims=True) + EPSILON)
    unit = centered * root
    scaled = normed_grad * gain
    inner = jnp.mean(scaled * unit, -1, keepdims=True)
    input_part = root * (scaled - jnp.mean(scaled, -1, keepdims=True) - unit * inner)
    grad_share = shared_rows(cotangent).astype(F32)
    tokens_grad = (grad_share + input_part).astype(BF16)
    norm_sums = jnp.stack([jnp.sum(normed_grad * unit, 0), jnp.sum(normed_grad, 0)])
    order.mark(norm_sums)
    order.mark(tokens_grad)
    small_sums = [norm_sums.reshape(1, -1), bias_sum] + [part[2] for part in fed_parts]
    small_sums = jnp.concatenate(small_sums + [qkv_bias_sum], 1)
    small_other = to_context(small_sums, 1)
    second_sum.far[0], first_sum.far[1] = arrived(second_sum.far[0], first_sum.far[1])
    second_sum.over_fsdp(1, second_sum.far[0])
    second_sum.over_chips(0)
    first_sum.over_cores(1)
    second_sum.far[1], second_sum.far[0], small_other = arrived(
        second_sum.far[1], second_sum.far[0], small_other
    )
    small_sums = small_sums + small_other
    small_other = to_fsdp(small_sums)
    last_sum.over_fsdp(1, second_sum.far[1])
    second_sum.over_chips(1)
    second_sum.over_cores(0)
    small_sums = small_sums + order.wait(small_other)[0]
    for mask in masks_of(across):
        small_sums = small_sums + to_context(small_sums, 2 * mask)
    norm_sums = order.mark(small_sums)[0, : 2 * width].reshape(2, width)
    high = norm_sums.astype(BF16)
    low = (norm_sums - high.astype(F32)).astype(BF16)
    extra = jnp.concatenate([high, low, jnp.zeros((12, width), BF16)], 0)
    gathered = jnp.concatenate([order(tokens_grad), extra], 0)
    gathered = lax.all_gather(gathered, "tensor", axis=0, tiled=False)
    tokens_grad = from_shares(gathered[:, :share])
    norm_sums = jnp.sum(gathered[:, share : share + 4].astype(F32), 0)
    norm_sums = norm_sums[:2] + norm_sums[2:]
    fc1_grad = order.mark(
        finish(place_s, [first_sum.pieces[0], second_sum.pieces[0]], block)
    )
    last_sum.far[1], second_sum.far[1] = arrived(last_sum.far[1], second_sum.far[1])
    last_sum.over_fsdp(0, last_sum.far[1])
    last_sum.over_chips(1)
    second_sum.over_cores(1)
    fc2_grad = order.mark(
        finish(place_s, [first_sum.pieces[1], second_sum.pieces[1]], block, turned=True)
    )
    (last_sum.far[0],) = arrived(last_sum.far[0])
    last_sum.over_chips(0)
    last_sum.over_cores(1)
    qkv_grad = order.mark(finish(place_s, [last_sum.pieces[1]], block, groups=3))
    last_sum.over_cores(0)
    out_grad = order.mark(finish(place_s, [last_sum.pieces[0]], block, turned=True))
    units_here = b_fc1.shape[0] * 2
    small_sums = small_sums[0]
    other_sums = small_sums[2 * width :]

    def shard_of(value):
        part = value.shape[-1] // 2
        return lax.dynamic_slice_in_dim(value, shard * part, part, value.ndim - 1)

    out_bias_grad = shard_of(other_sums[:width])
    fc1_bias_grad = shard_of(other_sums[width : width + units_here])
    qkv_bias_grad = shard_of(other_sums[width + units_here :].reshape(3, heads_width))
    return (
        block_out,
        tokens_grad,
        shard_of(norm_sums[0]),
        shard_of(norm_sums[1]),
        qkv_grad,
        qkv_bias_grad,
        out_grad,
        out_bias_grad,
        fc1_grad,
        fc1_bias_grad,
        fc2_grad,
        out_bias_grad,
    )


def solution(mesh):
    return jax.shard_map(
        per_device,
        mesh=mesh,
        in_specs=(
            P("fsdp", "context", None),
            P("fsdp"),
            P("fsdp"),
            P(None, "fsdp", "tensor"),
            P(None, ("tensor", "fsdp")),
            P("tensor", "fsdp"),
            P("fsdp"),
            P("fsdp", "tensor"),
            P(("tensor", "fsdp")),
            P("tensor", "fsdp"),
            P("fsdp"),
            P("fsdp", "context", None),
        ),
        out_specs=(
            P("fsdp", "context", None),
            P("fsdp", "context", None),
            P("fsdp"),
            P("fsdp"),
            P(None, "fsdp", "tensor"),
            P(None, ("tensor", "fsdp")),
            P("tensor", "fsdp"),
            P("fsdp"),
            P("fsdp", "tensor"),
            P(("tensor", "fsdp")),
            P("tensor", "fsdp"),
            P("fsdp"),
        ),
        check_vma=False,
    )
```
